128 devices in a mesh: lon: 8 (over z_lo, x), lat: 16 (over y, z_hi, core).
Axes of the slice: x: 4, y: 4, z: 4 (z_hi: 2, z_lo: 2; z = z_hi * 2 + z_lo), core: 2. Of those that a mesh axis runs over, the one named last changes fastest.
Arguments:
- tracers: float32 [2, 16, 256, 2048], P(None, None, 'lat', 'lon'), may hold values from -6 to 6
- east_velocity: float32 [16, 256, 2048], P(None, 'lat', 'lon'), may hold values from -0.3 to 0.3
- north_velocity: float32 [16, 256, 2048], P(None, 'lat', 'lon'), may hold values from -0.3 to 0.3
- ocean_levels: int32 [256, 2048], P('lat', 'lon'), may hold values from 0 to 16
- fold_partner: int32 [2048], P('lon'), may hold values from 0 to 2047, as said below
- atm_flux: float32 [2, 65536], P(None, ('lon', 'lat')), may hold values from -6 to 6
- remap_index: int32 [4, 256, 2048], P(None, 'lat', 'lon'), may hold values from 0 to 65535
- remap_weight: float32 [4, 256, 2048], P(None, 'lat', 'lon'), may hold values from 0 to 0.5
Outputs:
- tracers_out: float32 [2, 16, 256, 2048], P(None, None, 'lat', 'lon')
The draws below stay inside these ranges and needn't reach their ends.
Inputs may be any that keep to these rules, and one draw needn't show every extreme that they name: `fold_partner`: the partners of the columns of longitude tile t (global column i lies in tile i // 256) lie among the 512 columns of tiles (7 - t) mod 8 and (8 - t) mod 8; both of these tiles hold partners of tile t.
All inputs are finite; a program needn't handle non-finite values.
Results may differ from the reference program's by a relative error of at most 0.0003.
Values sent between devices are 32-bit elements; how exact they have to be, the bound alone decides.
No kernel may reach another device: no remote copies, remote signals or barrier semaphores. Data moves between devices by JAX's collectives and lax.ppermute only.
A program may use at most 128 MiB of HBM per device.

```python
import jax
import jax.numpy as jnp

K = 16
CX = 256
STEPS = 3
NW = 4
NX = 2048
NY = 256
NA = 65536


def pick_tile(single, tile_place, tile_count):
    mirror_start = jnp.remainder(tile_count - 1 - tile_place, tile_count) * CX
    turned_start = jnp.remainder(tile_count - tile_place, tile_count) * CX
    fixed_pair = jnp.stack([mirror_start + CX - 1, turned_start]).astype(jnp.int32)
    others = jnp.concatenate([mirror_start + jnp.arange(CX - 1), turned_start + 1 + jnp.arange(CX - 1)]).astype(jnp.int32)
    first_key, second_key = jax.random.split(single)
    others = jax.random.permutation(first_key, others)[:CX - 2]
    chosen = jnp.concatenate([fixed_pair, others])
    return jax.random.permutation(second_key, chosen)


def draw_fold_partner(key, part):
    key = jax.random.fold_in(key, 11)
    tile_count = NX // CX
    keys_all = jax.random.split(key, tile_count)
    tile_places = jnp.arange(tile_count).astype(jnp.int32)
    chosen = jax.vmap(lambda single, place: pick_tile(single, place, tile_count))(keys_all, tile_places)
    return chosen.reshape(NX).astype(jnp.int32)


def touch_ends(result, own_key, smallest, high):
    spot = [jax.random.randint(jax.random.fold_in(own_key, axis), (), 0, length) for axis, length in enumerate(result.shape)]
    longest = result.shape.index(max(result.shape))
    beside = spot[:longest] + [(spot[longest] + 1) % result.shape[longest]] + spot[longest + 1:]
    return result.at[tuple(spot)].set(smallest).at[tuple(beside)].set(high)


def shard_levels(stream_key, dims, shards, smallest, high):
    def one(dim, shards_of):
        draws = jax.random.uniform(jax.random.fold_in(jax.random.fold_in(stream_key, 6), dim), (shards_of,), jnp.float32, smallest / len(shards), high / len(shards))
        return jnp.repeat(jnp.exp(draws), dims[dim] // shards_of).reshape((-1,) + (1,) * (len(dims) - dim - 1))

    gain = one(*shards[0])
    for cut in shards[1:]:
        gain = gain * one(*cut)
    return gain


def normal_values(rng, shape, scale, reach, cuts=(), kind=jnp.bfloat16):
    factor_of = shard_levels(rng, shape, cuts, -0.22, 0.18) if cuts else 1.0
    drawn = jax.random.normal(rng, shape, jnp.float32) * scale * factor_of
    return jnp.minimum(jnp.maximum(drawn, -reach), reach).astype(kind)


def setup_inputs(seed: int = 0) -> dict:
    splits = jax.random.split(jax.random.key(seed), 9)
    return {
        "tracers": normal_values(splits[0], (2, K, NY, NX), 1.0, 6.0, ((2, 16), (3, 8)), jnp.float32),
        "east_velocity": jnp.clip(jax.random.uniform(splits[1], (K, NY, NX), jnp.float32, -0.3, 0.3) * shard_levels(splits[1], (K, NY, NX), ((1, 16), (2, 8)), -0.4, 0.0), -0.3, 0.3),
        "north_velocity": jnp.clip(jax.random.uniform(splits[2], (K, NY, NX), jnp.float32, -0.3, 0.3) * shard_levels(splits[2], (K, NY, NX), ((1, 16), (2, 8)), -0.4, 0.0), -0.3, 0.3),
        "ocean_levels": touch_ends(jax.random.randint(splits[3], (NY, NX), 0, K + 1), jax.random.fold_in(splits[3], 1), 0, K).astype(jnp.int32),
        "fold_partner": draw_fold_partner(jax.random.fold_in(splits[8], 71), 0),
        "atm_flux": normal_values(splits[5], (2, NA), 1.0, 6.0, ((1, 128),), jnp.float32),
        "remap_index": touch_ends(jax.random.randint(splits[6], (NW, NY, NX), 0, NA), jax.random.fold_in(splits[6], 1), 0, NA - 1).astype(jnp.int32),
        "remap_weight": jnp.clip(0.5 * jax.random.uniform(splits[7], (NW, NY, NX), jnp.float32) ** shard_levels(splits[7], (NW, NY, NX), ((1, 16), (2, 8)), -0.2, 0.2), 0.0, 0.5),
    }


def laplace(values_in, east_mask, north_mask):
    east_flux = east_mask * (values_in[..., 1:] - values_in[..., :-1])
    north_flux = north_mask * (values_in[..., 1:, :] - values_in[..., :-1, :])
    return (east_flux[..., 1:-1, 1:] - east_flux[..., 1:-1, :-1]) + (north_flux[..., 1:, 1:-1] - north_flux[..., :-1, 1:-1])


def advance(extended, wet_mask, east_ext, north_ext, surface):
    east_mask = wet_mask[..., :-1] * wet_mask[..., 1:]
    north_mask = wet_mask[:, :-1, :] * wet_mask[:, 1:, :]
    lap_once = laplace(extended, east_mask, north_mask)
    inner_east = east_mask[:, 1:-1, 1:-1]
    inner_north = north_mask[:, 1:-1, 1:-1]
    lap_twice = laplace(lap_once, inner_east, inner_north)
    near_cells = extended[..., 1:-1, 1:-1]
    east_flux = east_ext[:, 1:-1, 1:-2] * inner_east * 0.5 * (near_cells[..., :-1] + near_cells[..., 1:])
    north_flux = north_ext[:, 1:-2, 1:-1] * inner_north * 0.5 * (near_cells[..., :-1, :] + near_cells[..., 1:, :])
    spread = (east_flux[..., 1:-1, 1:] - east_flux[..., 1:-1, :-1]) + (north_flux[..., 1:, 1:-1] - north_flux[..., :-1, 1:-1])
    centre_cells = extended[..., 2:-2, 2:-2]
    wet_cells = wet_mask[:, 2:-2, 2:-2]
    vert_mask = wet_cells[:-1] * wet_cells[1:]
    vert_flux = vert_mask * (centre_cells[:, 1:] - centre_cells[:, :-1])
    zero_level = jnp.zeros_like(centre_cells[:, :1])
    vertical = jnp.concatenate([vert_flux, zero_level], axis=1) - jnp.concatenate([zero_level, vert_flux], axis=1)
    forcing = jnp.concatenate([surface[:, None], jnp.zeros_like(centre_cells[:, 1:])], axis=1)
    tendency = -spread + 0.08 * lap_once[..., 1:-1, 1:-1] - 0.01 * lap_twice + 0.1 * vertical + 0.5 * forcing
    return centre_cells + wet_cells * tendency


def extend_static(values_in, north_value):
    south_rows = jnp.zeros_like(values_in[:, :2])
    north_rows = jnp.full_like(values_in[:, :2], north_value)
    rows_all = jnp.concatenate([south_rows, values_in, north_rows], axis=1)
    return jnp.concatenate([rows_all[..., -2:], rows_all, rows_all[..., :2]], axis=2)


def extend_tracer(tracer, partner):
    ghost_rows = jnp.stack([tracer[:, :, -1], tracer[:, :, -2]], axis=2)
    ghost_rows = jnp.take(ghost_rows, partner, axis=3)
    south_rows = jnp.zeros_like(tracer[:, :, :2])
    rows_all = jnp.concatenate([south_rows, tracer, ghost_rows], axis=2)
    return jnp.concatenate([rows_all[..., -2:], rows_all, rows_all[..., :2]], axis=3)


def reference(tracers, east_velocity, north_velocity, ocean_levels, fold_partner, atm_flux, remap_index, remap_weight):
    levels = tracers.shape[1]
    north_fixed = north_velocity.at[:, -1, :].set(0.0)
    east_ext = extend_static(east_velocity, 0.0)
    north_ext = extend_static(north_fixed, 0.0)
    depth_float = ocean_levels.astype(tracers.dtype)[None]
    depth_ext = extend_static(depth_float, float(levels))[0]
    level_index = jnp.arange(levels).astype(tracers.dtype)
    wet_mask = (level_index[:, None, None] < depth_ext[None]).astype(tracers.dtype)
    surface = jnp.sum(remap_weight[None] * jnp.take(atm_flux, remap_index, axis=1), axis=1)
    tracer = tracers
    for repeat in range(STEPS):
        tracer = advance(extend_tracer(tracer, fold_partner), wet_mask, east_ext, north_ext, surface)
    return tracer
```

```python
import functools

import jax
import jax.numpy as jnp
from jax import lax
from jax.experimental import pallas as pl
from jax.experimental.pallas import tpu as pltpu
from jax.sharding import PartitionSpec as P

STEPS = 3
H = 8
VMEM = pl.BlockSpec(memory_space=pltpu.VMEM)
SMEM = pl.BlockSpec(memory_space=pltpu.SMEM)
PARAMS = pltpu.CompilerParams(vmem_limit_bytes=48 * 2**20)
F32 = jnp.float32
LANE_GATHER = lax.GatherDimensionNumbers(
    offset_dims=(),
    collapsed_slice_dims=(1,),
    start_index_map=(1,),
    operand_batching_dims=(0,),
    start_indices_batching_dims=(0,),
)


def lane_gather(values, lanes):
    return lax.gather(
        values, lanes[..., None], LANE_GATHER, (1, 1), mode=lax.GatherScatterMode.PROMISE_IN_BOUNDS
    )


def pick_columns(partner, sources):
    lanes = jnp.bitwise_and(partner, 127)
    place = jnp.right_shift(partner, 7)
    result = jnp.zeros((8, 128), F32)
    for tile, rows in sources:
        for half in range(2):
            got = lane_gather(rows[:, 128 * half : 128 * half + 128], lanes)
            result = jnp.where(place == 2 * tile + half, got, result)
    return result


def iota(shape, axis):
    return lax.broadcasted_iota(jnp.int32, shape, axis)


def pack_kernel(info, tracers, east, north, levels, weights, indices, partner, from_south, from_north, fold_a, fold_b, ghosts, to_west, to_east):
    tile, is_top = info[0], info[1] == 1
    wanted = jnp.broadcast_to(partner[...], (8, 256))
    for block in range(8):
        rows = pl.ds(8 * block, 8)
        sources = [(info[2], fold_a[rows, :]), (info[3], fold_b[rows, :])]
        for half in range(2):
            cut = slice(128 * half, 128 * half + 128)
            ghosts[rows, cut] = pick_columns(wanted[:, cut], sources)
    lane = iota((32, 128), 1)
    row = iota((32, 128), 0)
    ghost_first = jnp.logical_and(row == 24, is_top)
    ghost_second = jnp.logical_and(row == 25, is_top)
    last_north = jnp.logical_and(row == 23, is_top)
    beyond = jnp.logical_and(row >= 24, is_top)
    west_cut, east_cut = slice(0, 128), slice(128, 256)

    def whole(plane, centre, cut):
        return jnp.concatenate([from_south[plane, :, cut], centre, from_north[plane, :, cut]], axis=0)

    def value(plane, cut):
        if plane < 32:
            got = whole(plane, tracers[plane // 16, plane % 16, :, cut], cut)
            got = jnp.where(ghost_first, ghosts[plane : plane + 1, cut], got)
            return jnp.where(ghost_second, ghosts[32 + plane : 33 + plane, cut], got)
        if plane < 48:
            return whole(plane, east[plane - 32, :, cut], cut)
        if plane < 64:
            return jnp.where(last_north, 0.0, whole(plane, north[plane - 48, :, cut], cut))
        if plane < 68:
            return whole(plane, weights[plane - 64, :, cut], cut)
        if plane < 72:
            return whole(plane, indices[plane - 68, :, cut].astype(F32), cut)
        if plane == 72:
            return jnp.where(beyond, 16.0, whole(plane, levels[:, cut].astype(F32), cut))
        return jnp.broadcast_to(partner[:, cut].astype(F32), (32, 128))

    for group in range(5):
        first = jnp.zeros((32, 128), F32)
        last = jnp.zeros((32, 128), F32)
        for slot in range(16 if group < 4 else 10):
            mine = jnp.logical_and(lane >= 8 * slot, lane < 8 * slot + 8)
            plane = 16 * group + slot
            near = value(plane, west_cut)
            far = value(plane, east_cut)
            first = jnp.where(mine, pltpu.roll(near, 8 * slot, 1) if slot else near, first)
            last = jnp.where(mine, pltpu.roll(far, (8 * slot + 8) % 128, 1) if slot != 15 else far, last)
        to_west[group] = first
        to_east[group] = last


def one_hot_lookup(split_table, high, low, count):
    chosen = (iota((512, count), 0) == high).astype(F32).astype(jnp.bfloat16)
    got = jnp.dot(split_table[...], chosen, preferred_element_type=F32)
    lanes = iota((128, count), 0) == low
    first = jnp.sum(jnp.where(lanes, got[:128] + got[128:256], 0.0), axis=0, keepdims=True)
    second = jnp.sum(jnp.where(lanes, got[256:384] + got[384:], 0.0), axis=0, keepdims=True)
    return first, second


def split_place(index):
    high = jnp.bitwise_and(jnp.right_shift(index, 7), 3) * 128 + jnp.right_shift(index, 9)
    return high, jnp.bitwise_and(index, 127)


def lookup_kernel(table, weights, indices, from_south, from_north, surface, split_table, high, low, weight):
    for tracer in range(2):
        for quarter in range(4):
            block = table[:, tracer * 4 + quarter, :].T
            top = block.astype(jnp.bfloat16)
            rest = (block - top.astype(F32)).astype(jnp.bfloat16)
            cut = slice(128 * quarter, 128 * quarter + 128)
            split_table[tracer * 256 : tracer * 256 + 128, cut] = top
            split_table[tracer * 256 + 128 : tracer * 256 + 256, cut] = rest
    for j in range(4):
        index = jnp.concatenate(
            [from_south[68 + j].astype(jnp.int32), indices[j], from_north[68 + j].astype(jnp.int32)], axis=0
        )
        high[j], low[j] = split_place(index)
        weight[j] = jnp.concatenate([from_south[64 + j], weights[j], from_north[64 + j]], axis=0)
    surface[...] = jnp.zeros((2, 32, 256), F32)

    def body(step, carry):
        group, j = step // 4, step % 4
        rows = [pl.ds(4 + 4 * group + i, 1) for i in range(4)]
        join = lambda ref: jnp.concatenate([ref[j, r, :] for r in rows], axis=1)
        pair = one_hot_lookup(split_table, join(high), join(low), 1024)
        for i, r in enumerate(rows):
            scale = weight[j, r, :]
            for tracer in range(2):
                surface[tracer, r, :] += scale * pair[tracer][:, 256 * i : 256 * i + 256]
        return carry

    lax.fori_loop(0, 24, body, 0)


def spread_rows(halo, row_of, lane):
    moved = jnp.where(lane < 8, pltpu.roll(halo, 4, 1), jnp.zeros_like(halo))
    for shift in (8, 16, 32, 64):
        moved = moved + pltpu.roll(moved, shift, 1)
    return jnp.sum(jnp.where(lane // 8 == row_of, moved, jnp.zeros_like(moved)), axis=0, keepdims=True)


def gather_rows(packed, row_of, lane):
    moved = jnp.where(lane // 8 == row_of, jnp.broadcast_to(packed, (16, 128)), 0.0)
    for shift in (8, 16, 32, 64):
        moved = moved + pltpu.roll(moved, shift, 1)
    return pltpu.roll(moved, 124, 1)


def east_of(f):
    return pltpu.roll(f, f.shape[1] - 1, 1)


def west_of(f):
    return pltpu.roll(f, 1, 1)


def north_of(f):
    return pltpu.roll(f, f.shape[0] - 1, 0)


def south_of(f):
    return pltpu.roll(f, 1, 0)


def level_step(k, cells, upper, below_flux, coefficients, forcing):
    wet, vert_mask, east_mask, north_mask, east_near, east_far, north_near, north_far = coefficients
    cells_east, cells_north = east_of(cells), north_of(cells)
    grad_east = east_mask * (cells_east - cells)
    grad_north = north_mask * (cells_north - cells)
    lap = grad_east - west_of(grad_east) + (grad_north - south_of(grad_north))
    flux_east = east_far * cells_east - east_near * cells - (0.01 * east_mask) * (east_of(lap) - lap)
    flux_north = north_far * cells_north - north_near * cells - (0.01 * north_mask) * (north_of(lap) - lap)
    vert_flux = vert_mask * (upper - cells)
    tendency = flux_east - west_of(flux_east) + (flux_north - south_of(flux_north)) + 0.1 * (vert_flux - below_flux)
    if forcing is not None:
        tendency = tendency + forcing
    return cells + wet * tendency, vert_flux


def coefficients_of(k, depth, east_depth, north_depth, east, north):
    level = k.astype(F32) if hasattr(k, "astype") else float(k)
    one = lambda mask: mask.astype(F32)
    wet, vert_mask = one(level < depth), one(level + 1.0 < depth)
    east_mask, north_mask = one(level < east_depth), one(level < north_depth)
    half_east, half_north = 0.5 * east, 0.5 * north
    return (
        wet,
        vert_mask,
        east_mask,
        north_mask,
        east_mask * (0.08 + half_east),
        east_mask * (0.08 - half_east),
        north_mask * (0.08 + half_north),
        north_mask * (0.08 - half_north),
    )


def run_levels(load, depth, east_all, north_all, surface, store):
    east_depth = jnp.minimum(depth, east_of(depth))
    north_depth = jnp.minimum(depth, north_of(depth))
    shape = depth.shape

    def body(k, fluxes):
        coefficients = coefficients_of(k, depth, east_depth, north_depth, east_all[k], north_all[k])
        at_surface = jnp.where(k == 0, 0.5, 0.0).astype(F32)
        results = []
        for tracer in range(2):
            cells = load(tracer, k)
            upper = load(tracer, jnp.minimum(k + 1, 15))
            fresh, flux = level_step(k, cells, upper, fluxes[tracer], coefficients, at_surface * surface[tracer])
            store(tracer, k, fresh)
            results.append(flux)
        return tuple(results)

    lax.fori_loop(0, 16, body, (jnp.zeros(shape, F32), jnp.zeros(shape, F32)))


def first_kernel(
    info, tracers, east, north, levels, weights, indices, partner, from_south, from_north, ghosts, from_east, from_west,
    surface_main, split_table, cells_out, fold_out, east_ext, north_ext, depth_ext, surface_ext, partner_ext, start,
):
    is_top = info[1] == 1
    lane = iota((32, 128), 1)
    row = iota((32, 256), 0)
    last_north = jnp.logical_and(row == 23, is_top)

    def halo(group, slot):
        shift = (lambda v: v % 128) if isinstance(slot, int) else (lambda v: lax.rem(v, 128))
        near = pltpu.roll(from_east[group], shift(128 - 8 * slot), 1)
        far = pltpu.roll(from_west[group], shift(248 - 8 * slot), 1)
        return jnp.where(lane < 8, near, jnp.where(lane >= 120, far, 0.0))

    def whole(plane, centre):
        return jnp.concatenate([from_south[plane], centre, from_north[plane]], axis=0)

    def fill(k, carry):
        for tracer in range(2):
            start[tracer, k, :, 0:256] = whole(tracer * 16 + k, tracers[tracer, k])
            start[tracer, k, :, 256:384] = halo(tracer, k)
        east_ext[k, :, 0:256] = whole(32 + k, east[k])
        east_ext[k, :, 256:384] = halo(2, k)
        north_ext[k, :, 0:256] = jnp.where(last_north, 0.0, whole(48 + k, north[k]))
        north_ext[k, :, 256:384] = halo(3, k)
        return carry

    lax.fori_loop(0, 16, fill, 0)

    @pl.when(is_top)
    def _():
        def place(k, carry):
            for tracer in range(2):
                for r in range(2):
                    start[tracer, k, 24 + r : 25 + r, 0:256] = ghosts[pl.ds(32 * r + 16 * tracer + k, 1), :]
            return carry

        lax.fori_loop(0, 16, place, 0)

    depth_ext[:, 0:256] = jnp.where(
        jnp.logical_and(row >= 24, is_top), 16.0, whole(72, levels[...].astype(F32))
    )
    depth_ext[:, 256:384] = halo(4, 8)
    partner_ext[:, 0:256] = jnp.broadcast_to(partner[...], (8, 256))
    partner_ext[:, 256:384] = halo(4, 9)[0:8].astype(jnp.int32)

    small_lane, small_row = iota((16, 128), 1), iota((16, 128), 0)
    places, scales = [], []
    for j in range(4):
        index, weight = halo(4, 4 + j), halo(4, j)
        for part in range(2):
            cut = slice(16 * part, 16 * part + 16)
            places.append(spread_rows(index[cut], small_row, small_lane).astype(jnp.int32))
            scales.append(spread_rows(weight[cut], small_row, small_lane))
    high, low = split_place(jnp.concatenate(places, axis=1))
    pair = one_hot_lookup(split_table, high, low, 1024)
    surface_ext[:, :, 0:256] = surface_main[...]
    for tracer in range(2):
        for part in range(2):
            total = jnp.zeros((1, 128), F32)
            for j in range(4):
                at = 2 * j + part
                total += scales[at] * pair[tracer][:, 128 * at : 128 * at + 128]
            surface_ext[tracer, 16 * part : 16 * part + 16, 256:384] = gather_rows(total, small_row, small_lane)

    def store(tracer, k, fresh):
        cells_out[tracer, k] = fresh
        for r in range(2):
            fold_out[pl.ds(32 * r + 16 * tracer + k, 1), :] = fresh[23 - r : 24 - r, 0:256]

    surfaces = [surface_ext[0], surface_ext[1]]
    run_levels(lambda tracer, k: start[tracer, k], depth_ext[...], east_ext, north_ext, surfaces, store)


def next_kernel(last, info, cells, east_ext, north_ext, depth_ext, surface_ext, partner_ext, fold_a, fold_b, fold_c, fold_d, *outs):
    if last:
        cells_out, ghosts = outs
    else:
        cells_out, fold_out, ghosts = outs
    is_top = info[1] == 1

    @pl.when(is_top)
    def _():
        def block_body(block, carry):
            rows = pl.ds(pl.multiple_of(8 * block, 8), 8)
            near = [(info[2], fold_a[rows, :]), (info[3], fold_b[rows, :])]
            wide = near + [(info[4], fold_c[rows, :]), (info[5], fold_d[rows, :])]
            for part, sources in enumerate((near, near, wide)):
                cut = slice(128 * part, 128 * part + 128)
                ghosts[rows, cut] = pick_columns(partner_ext[:, cut], sources)
            return carry

        lax.fori_loop(0, 8, block_body, 0)

    row = iota((32, 384), 0)
    ghost_first = jnp.logical_and(row == 24, is_top)
    ghost_second = jnp.logical_and(row == 25, is_top)

    def load(tracer, k):
        plane = 16 * tracer + k
        got = cells[tracer, k]
        got = jnp.where(ghost_first, ghosts[pl.ds(plane, 1), :], got)
        return jnp.where(ghost_second, ghosts[pl.ds(32 + plane, 1), :], got)

    def store(tracer, k, fresh):
        if last:
            cells_out[tracer, k] = fresh[8:24, 0:256]
        else:
            cells_out[tracer, k] = fresh
            for r in range(2):
                fold_out[pl.ds(32 * r + 16 * tracer + k, 1), :] = fresh[23 - r : 24 - r, 0:256]

    surfaces = [surface_ext[0], surface_ext[1]]
    run_levels(load, depth_ext[...], east_ext, north_ext, surfaces, store)


def call(kernel, ins, outs, scratch=(), cost=None):
    return pl.pallas_call(
        kernel,
        out_shape=tuple(jax.ShapeDtypeStruct(s, d) for s, d in outs),
        in_specs=[SMEM if i == 0 and v.shape == (6,) else VMEM for i, v in enumerate(ins)],
        out_specs=tuple(VMEM for _ in outs),
        scratch_shapes=list(scratch),
        compiler_params=PARAMS,
        cost_estimate=cost,
    )(*ins)


def per_device(tracers, east, north, levels, partner, atm_flux, indices, weights):
    nlon, nlat = lax.axis_size("lon"), lax.axis_size("lat")
    both = ("lon", "lat")
    t, lat = lax.axis_index("lon"), lax.axis_index("lat")
    is_top = (lat == nlat - 1).astype(jnp.int32)
    tiles = [jnp.remainder(nlon - 1 - t + d, nlon) for d in (0, 1, -1, 2)]
    info = jnp.stack([t, is_top] + tiles).astype(jnp.int32)
    top = nlat - 1

    def fold_permutes(rows, shifts):
        return [
            lax.ppermute(rows, both, [(i * nlat + top, ((nlon - 1 + d - i) % nlon) * nlat + top) for i in range(nlon)])
            for d in shifts
        ]

    def cut(a, rows):
        return a[..., rows, :].reshape((-1, H, a.shape[-1])).astype(F32)

    pieces = (tracers, east, north, weights, indices, levels)
    northward = jnp.concatenate([cut(a, slice(8, 16)) for a in pieces], axis=0)
    southward = jnp.concatenate([cut(a, slice(0, 8)) for a in pieces], axis=0)
    from_south = lax.ppermute(northward, "lat", [(i, i + 1) for i in range(nlat - 1)])
    from_north = lax.ppermute(southward, "lat", [(i + 1, i) for i in range(nlat - 1)])
    fold_rows = jnp.concatenate(
        [tracers[:, :, 15].reshape(32, -1), tracers[:, :, 14].reshape(32, -1)], axis=0
    )
    fold_a, fold_b = fold_permutes(fold_rows, (0, 1))

    block = atm_flux.reshape(8, 128)
    slots = jnp.broadcast_to(block[None], (nlon * nlat, 8, 128))
    table = lax.all_to_all(slots, both, 0, 0, tiled=True)

    partner_row = partner.reshape(1, -1)
    ghosts, to_west, to_east = call(
        pack_kernel,
        (info, tracers, east, north, levels, weights, indices, partner_row, from_south, from_north, fold_a, fold_b),
        [((64, 256), F32), ((5, 32, 128), F32), ((5, 32, 128), F32)],
    )
    from_east = lax.ppermute(to_west, "lon", [((i + 1) % nlon, i) for i in range(nlon)])
    from_west = lax.ppermute(to_east, "lon", [(i, (i + 1) % nlon) for i in range(nlon)])

    surface, split_table = call(
        lookup_kernel,
        (table, weights, indices, from_south, from_north),
        [((2, 32, 256), F32), ((512, 512), jnp.bfloat16)],
        [pltpu.VMEM((4, 32, 256), jnp.int32), pltpu.VMEM((4, 32, 256), jnp.int32), pltpu.VMEM((4, 32, 256), F32)],
        pl.CostEstimate(flops=2 * 512 * 512 * 24576, bytes_accessed=4 * 2**20, transcendentals=0),
    )

    wide = (2, 16, 32, 384)
    cells, fold_rows, east_ext, north_ext, depth_ext, surface_ext, partner_ext = call(
        first_kernel,
        (info, tracers, east, north, levels, weights, indices, partner_row, from_south, from_north, ghosts, from_east,
         from_west, surface, split_table),
        [(wide, F32), ((64, 256), F32), (wide[1:], F32), (wide[1:], F32), ((32, 384), F32), ((2, 32, 384), F32),
         ((8, 384), jnp.int32)],
        [pltpu.VMEM(wide, F32)],
    )
    for step in range(1, STEPS):
        last = step == STEPS - 1
        received = fold_permutes(fold_rows, (0, 1, -1, 2))
        outs = call(
            functools.partial(next_kernel, last),
            (info, cells, east_ext, north_ext, depth_ext, surface_ext, partner_ext, *received),
            [(tracers.shape, F32)] if last else [(wide, F32), ((64, 256), F32)],
            [pltpu.VMEM((64, 384), F32)],
        )
        if last:
            return outs[0]
        cells, fold_rows = outs


def solution(mesh):
    return jax.shard_map(
        per_device,
        mesh=mesh,
        in_specs=(
            P(None, None, "lat", "lon"),
            P(None, "lat", "lon"),
            P(None, "lat", "lon"),
            P("lat", "lon"),
            P("lon"),
            P(None, ("lon", "lat")),
            P(None, "lat", "lon"),
            P(None, "lat", "lon"),
        ),
        out_specs=P(None, None, "lat", "lon"),
        check_vma=False,
    )
```

```python
import functools

import jax
import jax.numpy as jnp
from jax import lax
from jax.experimental import pallas as pl
from jax.experimental.pallas import tpu as pltpu
from jax.sharding import PartitionSpec as P

H = 8
VMEM = pl.BlockSpec(memory_space=pltpu.VMEM)
SMEM = pl.BlockSpec(memory_space=pltpu.SMEM)
PARAMS = pltpu.CompilerParams(vmem_limit_bytes=20 * 2**20)
F32 = jnp.float32
LANE_GATHER = lax.GatherDimensionNumbers(
    offset_dims=(),
    collapsed_slice_dims=(1,),
    start_index_map=(1,),
    operand_batching_dims=(0,),
    start_indices_batching_dims=(0,),
)


def lane_gather(values, lanes):
    return lax.gather(
        values, lanes[..., None], LANE_GATHER, (1, 1), mode=lax.GatherScatterMode.PROMISE_IN_BOUNDS
    )


def pick_columns(partner, sources):
    lanes = jnp.bitwise_and(partner, 127)
    place = jnp.right_shift(partner, 7)
    result = jnp.zeros((8, 128), F32)
    for tile, rows in sources:
        for half in range(2):
            got = lane_gather(rows[:, 128 * half : 128 * half + 128], lanes)
            result = jnp.where(place == 2 * tile + half, got, result)
    return result


def iota(shape, axis):
    return lax.broadcasted_iota(jnp.int32, shape, axis)


def build_kernel(info, *refs):
    sources, (first, second, fold_rows, slots), held, done = refs[:7], refs[7:11], refs[11:18], refs[18]
    copies = [pltpu.make_async_copy(a, b, done.at[i]) for i, (a, b) in enumerate(zip(sources, held))]
    for copy in copies:
        copy.start()
    for copy in copies:
        copy.wait()
    tracers, east, north, levels, weights, indices, flux = held
    for tracer in range(2):
        for quarter in range(4):
            cut = flux[tracer : tracer + 1, 128 * quarter : 128 * quarter + 128]
            slots[:, 4 * tracer + quarter, :] = jnp.broadcast_to(cut, (128, 128))

    def write(out, rows):
        for tracer in range(2):
            out[16 * tracer : 16 * tracer + 16] = tracers[tracer, :, rows, :]
        out[32:48] = east[:, rows, :]
        out[48:64] = north[:, rows, :]
        out[64:68] = weights[:, rows, :]
        out[68:72] = indices[:, rows, :].astype(F32)
        out[72] = levels[rows, :].astype(F32)

    is_odd = info[6] == 1

    @pl.when(is_odd)
    def _():
        write(first, slice(0, 8))
        write(second, slice(8, 16))

    @pl.when(jnp.logical_not(is_odd))
    def _():
        write(first, slice(8, 16))
        write(second, slice(0, 8))

    for r in range(2):
        for tracer in range(2):
            at = 4 * r + 2 * tracer
            for part in range(2):
                fold_rows[at + part] = tracers[tracer, 8 * part : 8 * part + 8, 15 - r, :]
        wet = levels[15 - r : 16 - r, :] > 0
        for j in range(4):
            weight = weights[j, 15 - r : 16 - r, :]
            fold_rows[8 + r, j : j + 1, :] = jnp.where(wet, weight, jnp.zeros_like(weight))
            fold_rows[8 + r, 4 + j : 5 + j, :] = indices[j, 15 - r : 16 - r, :].astype(F32)

    @pl.when(info[1] == 1)
    def _():
        second[0:10] = fold_rows[...]


class Sides:
    def __init__(self, info, first, second):
        self.odd, self.top = info[6] == 1, info[1] == 1
        self.first, self.second = first, second

    def south(self, plane, cut=slice(None)):
        return jnp.where(self.odd, self.first[plane, :, cut], self.second[plane, :, cut])

    def north(self, plane, cut=slice(None)):
        got = jnp.where(self.odd, self.second[plane, :, cut], self.first[plane, :, cut])
        return jnp.where(self.top, 0.0, got)

    def whole(self, plane, centre, cut=slice(None)):
        return jnp.concatenate([self.south(plane, cut), centre, self.north(plane, cut)], axis=0)


def pack_kernel(info, tracers, east, north, levels, weights, indices, partner, first, second, fold_b, ghosts, to_west, to_east):
    is_top = info[1] == 1
    wanted = jnp.broadcast_to(partner[...], (8, 256))
    for block in range(10):
        rows = pl.ds(8 * block, 8)
        sources = [(info[2], second[block]), (info[3], fold_b[block])]
        for half in range(2):
            cut = slice(128 * half, 128 * half + 128)
            ghosts[rows, cut] = pick_columns(wanted[:, cut], sources)
    lane = iota((32, 128), 1)
    row = iota((32, 128), 0)
    ghost_first = jnp.logical_and(row == 24, is_top)
    ghost_second = jnp.logical_and(row == 25, is_top)
    last_north = jnp.logical_and(row == 23, is_top)
    beyond = jnp.logical_and(row >= 24, is_top)
    west_cut, east_cut = slice(0, 128), slice(128, 256)

    whole = Sides(info, first, second).whole

    def value(plane, cut):
        if plane < 32:
            got = whole(plane, tracers[plane // 16, plane % 16, :, cut], cut)
            got = jnp.where(ghost_first, ghosts[plane : plane + 1, cut], got)
            return jnp.where(ghost_second, ghosts[32 + plane : 33 + plane, cut], got)
        if plane < 48:
            return whole(plane, east[plane - 32, :, cut], cut)
        if plane < 64:
            return jnp.where(last_north, 0.0, whole(plane, north[plane - 48, :, cut], cut))
        if plane < 72:
            centre = weights[plane - 64, :, cut] if plane < 68 else indices[plane - 68, :, cut].astype(F32)
            got = jnp.where(ghost_first, ghosts[plane : plane + 1, cut], whole(plane, centre, cut))
            return jnp.where(ghost_second, ghosts[plane + 8 : plane + 9, cut], got)
        if plane == 72:
            return jnp.where(beyond, 16.0, whole(plane, levels[:, cut].astype(F32), cut))
        return jnp.broadcast_to(partner[:, cut].astype(F32), (32, 128))

    for group in range(5):
        westward = jnp.zeros((32, 128), F32)
        eastward = jnp.zeros((32, 128), F32)
        for slot in range(16 if group < 4 else 10):
            mine = jnp.logical_and(lane >= 8 * slot, lane < 8 * slot + 8)
            plane = 16 * group + slot
            near = value(plane, west_cut)
            far = value(plane, east_cut)
            westward = jnp.where(mine, pltpu.roll(near, 8 * slot, 1) if slot else near, westward)
            eastward = jnp.where(mine, pltpu.roll(far, (8 * slot + 8) % 128, 1) if slot != 15 else far, eastward)
        to_west[group] = westward
        to_east[group] = eastward


def one_hot_lookup(split_table, high, low, count):
    chosen = (iota((512, count), 0) == high).astype(F32).astype(jnp.bfloat16)
    got = jnp.dot(split_table[...], chosen, preferred_element_type=F32)
    lanes = iota((128, count), 0) == low
    first = jnp.sum(jnp.where(lanes, got[:128] + got[128:256], 0.0), axis=0, keepdims=True)
    second = jnp.sum(jnp.where(lanes, got[256:384] + got[384:], 0.0), axis=0, keepdims=True)
    return first, second


def split_place(index):
    high = jnp.bitwise_and(jnp.right_shift(index, 7), 3) * 128 + jnp.right_shift(index, 9)
    return high, jnp.bitwise_and(index, 127)


def split_kernel_table(table, split_table):
    for tracer in range(2):
        for quarter in range(4):
            block = table[:, tracer * 4 + quarter, :].T
            top = block.astype(jnp.bfloat16)
            rest = (block - top.astype(F32)).astype(jnp.bfloat16)
            cut = slice(128 * quarter, 128 * quarter + 128)
            split_table[tracer * 256 : tracer * 256 + 128, cut] = top
            split_table[tracer * 256 + 128 : tracer * 256 + 256, cut] = rest


def halo_tile(from_east, from_west, lane, group, slot):
    shift = (lambda v: v % 128) if isinstance(slot, int) else (lambda v: lax.rem(v, 128))
    near = pltpu.roll(from_east[group], shift(128 - 8 * slot), 1)
    far = pltpu.roll(from_west[group], shift(248 - 8 * slot), 1)
    return jnp.where(lane < 8, near, jnp.where(lane >= 120, far, 0.0))


def lookup_kernel(groups, splits, last, info, table, weights, indices, first, second, ghosts, *rest):
    if last:
        from_east, from_west, surface, halo_surface, high, low, weight = rest
    elif splits:
        surface, split_table, high, low, weight = rest
    else:
        surface, high, low, weight = rest
    if splits:
        split_kernel_table(table, split_table)
    else:
        split_table = table
    is_top = info[1] == 1
    whole = Sides(info, first, second).whole
    row = iota((32, 256), 0)
    for j in range(4):
        index = whole(68 + j, indices[j].astype(F32))
        scale = whole(64 + j, weights[j])
        for r in range(2):
            ghost = jnp.logical_and(row == 24 + r, is_top)
            scale = jnp.where(ghost, ghosts[64 + 8 * r + j : 65 + 8 * r + j, :], scale)
            index = jnp.where(ghost, ghosts[68 + 8 * r + j : 69 + 8 * r + j, :], index)
        high[j], low[j] = split_place(index.astype(jnp.int32))
        weight[j] = scale
    surface[...] = jnp.zeros(surface.shape, F32)
    start = 4 * groups[0]

    def body(step, carry):
        group, j = step // 4, step % 4
        rows = [4 * group + i for i in range(4)]
        join = lambda ref: jnp.concatenate([ref[j, pl.ds(start + r, 1), :] for r in rows], axis=1)
        pair = one_hot_lookup(split_table, join(high), join(low), 1024)
        for i, r in enumerate(rows):
            scale = weight[j, pl.ds(start + r, 1), :]
            for tracer in range(2):
                surface[tracer, pl.ds(r, 1), :] += scale * pair[tracer][:, 256 * i : 256 * i + 256]
        return carry

    lax.fori_loop(0, 4 * len(groups), body, 0, unroll=2)
    if last:
        lane = iota((32, 128), 1)
        small_lane, small_row = iota((16, 128), 1), iota((16, 128), 0)
        places, scales = [], []
        for j in range(4):
            index = halo_tile(from_east, from_west, lane, 4, 4 + j)
            scale = halo_tile(from_east, from_west, lane, 4, j)
            for part in range(2):
                cut = slice(16 * part, 16 * part + 16)
                places.append(spread_rows(index[cut], small_row, small_lane).astype(jnp.int32))
                scales.append(spread_rows(scale[cut], small_row, small_lane))
        halo_high, halo_low = split_place(jnp.concatenate(places, axis=1))
        pair = one_hot_lookup(split_table, halo_high, halo_low, 1024)
        for tracer in range(2):
            for part in range(2):
                total = jnp.zeros((1, 128), F32)
                for j in range(4):
                    at = 2 * j + part
                    total += scales[at] * pair[tracer][:, 128 * at : 128 * at + 128]
                halo_surface[tracer, 16 * part : 16 * part + 16, :] = gather_rows(total, small_row, small_lane)


def spread_rows(halo, row_of, lane):
    moved = jnp.where(lane < 8, pltpu.roll(halo, 4, 1), jnp.zeros_like(halo))
    for shift in (8, 16, 32, 64):
        moved = moved + pltpu.roll(moved, shift, 1)
    return jnp.sum(jnp.where(lane // 8 == row_of, moved, jnp.zeros_like(moved)), axis=0, keepdims=True)


def gather_rows(packed, row_of, lane):
    moved = jnp.where(lane // 8 == row_of, jnp.broadcast_to(packed, (16, 128)), 0.0)
    for shift in (8, 16, 32, 64):
        moved = moved + pltpu.roll(moved, shift, 1)
    return pltpu.roll(moved, 124, 1)


def east_of(f):
    return pltpu.roll(f, f.shape[1] - 1, 1)


def west_of(f):
    return pltpu.roll(f, 1, 1)


def north_of(f):
    return pltpu.roll(f, f.shape[0] - 1, 0)


def south_of(f):
    return pltpu.roll(f, 1, 0)


def run_levels(cells, half_east, half_north, depth, surface, store, window=slice(0, 32), keep=slice(0, 32), tracers=(0, 1)):
    depth = depth[window, :]
    east_depth = jnp.minimum(depth, east_of(depth))
    north_depth = jnp.minimum(depth, north_of(depth))
    kept = slice(window.start + keep.start, window.start + keep.stop)

    def body(k, carry):
        level = k.astype(F32)
        east_open, north_open, wet = level < east_depth, level < north_depth, level < depth[keep]
        deeper = level + 1.0 < depth[keep]
        east, north = half_east[k, window, :], half_north[k, window, :]
        above, under = jnp.minimum(k + 1, 15), jnp.maximum(k - 1, 0)
        at_surface = jnp.where(k == 0, 0.5, 0.0).astype(F32)
        for tracer in tracers:
            here = cells[tracer, k]
            to_east, to_north = east_of(here), north_of(here)
            grad_east = jnp.where(east_open, to_east - here, 0.0)
            grad_north = jnp.where(north_open, to_north - here, 0.0)
            lap = grad_east - west_of(grad_east) + (grad_north - south_of(grad_north))
            flat = 0.08 * here - 0.01 * lap
            flux_east = jnp.where(east_open, east_of(flat) - flat - east * (to_east + here), 0.0)
            flux_north = jnp.where(north_open, north_of(flat) - flat - north * (to_north + here), 0.0)
            total = (flux_east - west_of(flux_east) + (flux_north - south_of(flux_north)))[keep]
            centre = here[keep]
            vertical = jnp.where(deeper, cells[tracer, above, keep, :] - centre, 0.0)
            total += 0.1 * (vertical - (centre - cells[tracer, under, keep, :]))
            if surface is not None:
                total += at_surface * surface[tracer, kept, :]
            store(tracer, k, centre + jnp.where(wet, total, 0.0))
        return carry

    lax.fori_loop(0, 16, body, 0)


def keep_step(cells_out, fold_out):
    def store(tracer, k, fresh):
        cells_out[tracer, k] = fresh
        for r in range(2):
            fold_out[pl.ds(32 * r + 16 * tracer + k, 1), :] = fresh[23 - r : 24 - r, 0:256]

    return store


def place_ghosts(cells, ghosts, columns, row=24):
    def place(k, carry):
        for tracer in range(2):
            for r in range(2):
                cells[tracer, k, row + r : row + r + 1, 0:columns] = ghosts[pl.ds(32 * r + 16 * tracer + k, 1), :]
        return carry

    lax.fori_loop(0, 16, place, 0)


def first_kernel(
    info, tracers, east, north, levels, partner, first, second, ghosts, from_east, from_west,
    cells_out, fold_out, east_ext, north_ext, depth_ext, partner_ext, start,
):
    is_top = info[1] == 1
    lane = iota((32, 128), 1)
    row = iota((32, 256), 0)
    last_north = jnp.logical_and(row == 23, is_top)
    halo = functools.partial(halo_tile, from_east, from_west, lane)

    whole = Sides(info, first, second).whole

    def fill(k, carry):
        for tracer in range(2):
            start[tracer, k, :, 0:256] = whole(tracer * 16 + k, tracers[tracer, k])
            start[tracer, k, :, 256:384] = halo(tracer, k)
        east_ext[k, :, 0:256] = 0.5 * whole(32 + k, east[k])
        east_ext[k, :, 256:384] = 0.5 * halo(2, k)
        north_ext[k, :, 0:256] = jnp.where(last_north, 0.0, 0.5 * whole(48 + k, north[k]))
        north_ext[k, :, 256:384] = 0.5 * halo(3, k)
        return carry

    lax.fori_loop(0, 16, fill, 0)

    @pl.when(is_top)
    def _():
        place_ghosts(start, ghosts, 256)

    depth_ext[:, 0:256] = jnp.where(
        jnp.logical_and(row >= 24, is_top), 16.0, whole(72, levels[...].astype(F32))
    )
    depth_ext[:, 256:384] = halo(4, 8)
    partner_ext[:, 0:256] = jnp.broadcast_to(partner[...], (8, 256))
    partner_ext[:, 256:384] = halo(4, 9)[0:8].astype(jnp.int32)
    run_levels(start, east_ext, north_ext, depth_ext, None, keep_step(cells_out, fold_out))


def fold_ghosts(info, partner_ext, received, ghosts):
    def block_body(block, carry):
        rows = pl.ds(pl.multiple_of(8 * block, 8), 8)
        all_sources = [(info[2 + i], ref[rows, :]) for i, ref in enumerate(received)]
        for part, sources in enumerate((all_sources[:2], all_sources[:2], all_sources)):
            cut = slice(128 * part, 128 * part + 128)
            ghosts[rows, cut] = pick_columns(partner_ext[:, cut], sources)
        return carry

    lax.fori_loop(0, 8, block_body, 0)


def second_kernel(
    info, cells, east_ext, north_ext, depth_ext, partner_ext, fold_a, fold_b, fold_c, fold_d, surface_a, surface_b, surface_c, surface_d,
    surface_e, halo_surface, cells_out, fold_out, surface_ext, ghosts, start,
):
    def fill(k, carry):
        for tracer in range(2):
            start[tracer, k] = cells[tracer, k]
        return carry

    lax.fori_loop(0, 16, fill, 0)

    @pl.when(info[1] == 1)
    def _():
        fold_ghosts(info, partner_ext, (fold_a, fold_b, fold_c, fold_d), ghosts)
        place_ghosts(start, ghosts, 384)

    surface_ext[...] = jnp.zeros((2, 32, 384), F32)
    for tracer in range(2):
        at = 4
        for piece in (surface_a, surface_b, surface_c, surface_d, surface_e):
            surface_ext[tracer, at : at + piece.shape[1], 0:256] = piece[tracer]
            at += piece.shape[1]
        surface_ext[tracer, :, 256:384] = halo_surface[tracer]
        start[tracer, 0] = start[tracer, 0] + jnp.where(depth_ext[...] > 0.0, 0.5 * surface_ext[tracer], 0.0)
    run_levels(start, east_ext, north_ext, depth_ext, surface_ext, keep_step(cells_out, fold_out))


def last_kernel(
    info, cells, east_ext, north_ext, depth_ext, partner_ext, fold_a, fold_b, fold_c, fold_d, surface_ext, result, ghosts, start
):
    def fill(k, carry):
        for tracer in range(2):
            start[tracer, k] = cells[tracer, k]
        return carry

    lax.fori_loop(0, 16, fill, 0)

    @pl.when(info[1] == 1)
    def _():
        fold_ghosts(info, partner_ext, (fold_a, fold_b, fold_c, fold_d), ghosts)
        place_ghosts(start, ghosts, 384)

    def store(tracer, k, fresh):
        result[tracer, k] = fresh[:, 0:256]

    run_levels(start, east_ext, north_ext, depth_ext, surface_ext, store, keep=slice(8, 24))


def call(kernel, ins, outs, scratch=(), cost=None, earlier=(), ins_any=False, outs_any=False, alias=None, params=PARAMS):
    used = len(ins)

    def body(*refs):
        kernel(*refs[:used], *refs[used + len(earlier) :])

    anywhere = pl.BlockSpec(memory_space=pl.ANY)
    hbm = pl.BlockSpec(memory_space=pltpu.HBM)

    def place(i, v):
        if v.ndim == 1:
            return SMEM
        return hbm if ins_any or i == alias else anywhere if i >= used else VMEM

    arrays = tuple(ins) + tuple(earlier)
    return pl.pallas_call(
        body,
        out_shape=tuple(jax.ShapeDtypeStruct(s, d) for s, d in outs),
        in_specs=[place(i, v) for i, v in enumerate(arrays)],
        out_specs=tuple(hbm if outs_any else VMEM for _ in outs),
        scratch_shapes=list(scratch),
        compiler_params=params,
        cost_estimate=cost,
        input_output_aliases={} if alias is None else {alias: 0},
    )(*arrays)


STEP_COST = pl.CostEstimate(flops=10**7, bytes_accessed=16 * 2**20, transcendentals=0)


def lookup_cost(groups):
    return pl.CostEstimate(flops=groups * 2 * 512 * 512 * 4096, bytes_accessed=groups * 2**20, transcendentals=0)


def per_device(tracers, east, north, levels, partner, atm_flux, indices, weights):
    nlon, nlat = lax.axis_size("lon"), lax.axis_size("lat")
    both = ("lon", "lat")
    t, lat = lax.axis_index("lon"), lax.axis_index("lat")
    is_top = (lat == nlat - 1).astype(jnp.int32)
    tiles = [jnp.remainder(nlon - 1 - t + d, nlon) for d in (0, 1, -1, 2)]
    info = jnp.stack([t, is_top] + tiles + [lat % 2]).astype(jnp.int32)
    top = nlat - 1

    def fold_permute(rows, d):
        pairs = [(i * nlat + top, ((nlon - 1 + d - i) % nlon) * nlat + top) for i in range(nlon)]
        return lax.ppermute(rows, both, pairs)

    message = ((73, H, 256), F32)
    whole_inputs = (tracers, east, north, levels, weights, indices)
    build_inputs = (*whole_inputs, atm_flux)
    first, second, fold_rows, slots = call(
        build_kernel,
        (info, *build_inputs),
        [message, message, ((10, 8, 256), F32), ((nlon * nlat, 8, 128), F32)],
        [pltpu.VMEM(a.shape, a.dtype) for a in build_inputs] + [pltpu.SemaphoreType.DMA((7,))],
        ins_any=True,
        params=pltpu.CompilerParams(vmem_limit_bytes=60 * 2**20),
    )
    def after(value, *earlier):
        return lax.optimization_barrier((value, *earlier))[0]

    swaps = [(i, i + 1) for i in range(0, nlat, 2)]
    first = lax.ppermute(first, "lat", swaps + [(j, i) for i, j in swaps])
    swaps = [(i, i + 1) for i in range(1, nlat - 1, 2)]
    swaps = [(c * nlat + i, c * nlat + j) for c in range(nlon) for i, j in swaps + [(j, i) for i, j in swaps]]
    facing = [(c * nlat + top, (nlon - 1 - c) * nlat + top) for c in range(nlon)]
    second = lax.ppermute(second, both, swaps + facing)
    fold_b = fold_permute(fold_rows, 1)

    table = lax.all_to_all(slots, both, 0, 0, tiled=True)

    partner_row = partner.reshape(1, -1)
    ghosts, to_west, to_east = call(
        pack_kernel,
        (info, *whole_inputs, partner_row, first, second, fold_b),
        [((80, 256), F32), ((5, 32, 128), F32), ((5, 32, 128), F32)],
    )
    from_east = lax.ppermute(to_west, "lon", [((i + 1) % nlon, i) for i in range(nlon)])
    from_west = lax.ppermute(to_east, "lon", [(i, (i + 1) % nlon) for i in range(nlon)])

    def lookups(groups, table, splits=False, last=False, earlier=()):
        outs = [((2, 4 * len(groups), 256), F32)]
        outs += [((512, 512), jnp.bfloat16)] if splits else [((2, 32, 128), F32)] if last else []
        words = pltpu.VMEM((4, 32, 256), jnp.int32)
        return call(
            functools.partial(lookup_kernel, groups, splits, last),
            (info, table, weights, indices, first, second, ghosts) + ((from_east, from_west) if last else ()),
            outs,
            [words, words, pltpu.VMEM((4, 32, 256), F32)],
            lookup_cost(len(groups)),
            earlier,
        )

    surface_a, split_table = lookups((1, 2), table, splits=True)

    wide = (2, 16, 32, 384)
    cells, fold_rows, east_ext, north_ext, depth_ext, partner_ext = call(
        first_kernel,
        (info, tracers, east, north, levels, partner_row, first, second, ghosts, from_east, from_west),
        [(wide, F32), ((64, 256), F32), (wide[1:], F32), (wide[1:], F32), ((32, 384), F32), ((8, 384), jnp.int32)],
        [pltpu.VMEM(wide, F32)],
        STEP_COST,
        (surface_a,),
    )
    statics = (east_ext, north_ext, depth_ext)
    received = [fold_permute(fold_rows, 0)]
    (surface_b,) = lookups((3,), split_table, earlier=(fold_rows,))
    received.append(fold_permute(after(fold_rows, surface_b), 1))
    (surface_c,) = lookups((4,), split_table, earlier=(received[0], surface_b))
    received.append(fold_permute(after(fold_rows, surface_c), -1))
    (surface_d,) = lookups((5,), split_table, earlier=(received[1], surface_c))
    received.append(fold_permute(after(fold_rows, surface_d), 2))
    surface_e, halo_surface = lookups((6,), split_table, last=True, earlier=(received[2], surface_d))

    ghost_rows = pltpu.VMEM((64, 384), F32)
    cells, fold_rows, surface_ext = call(
        second_kernel,
        (info, cells, *statics, partner_ext, *received, surface_a, surface_b, surface_c, surface_d, surface_e,
         halo_surface),
        [(wide, F32), ((64, 256), F32), ((2, 32, 384), F32)],
        [ghost_rows, pltpu.VMEM(wide, F32)],
        STEP_COST,
    )
    received = [fold_permute(fold_rows, d) for d in (0, 1, -1, 2)]
    (result,) = call(
        last_kernel,
        (info, cells, *statics, partner_ext, *received, surface_ext),
        [(tracers.shape, F32)],
        [ghost_rows, pltpu.VMEM(wide, F32)],
        STEP_COST,
    )
    return result


def solution(mesh):
    return jax.shard_map(
        per_device,
        mesh=mesh,
        in_specs=(
            P(None, None, "lat", "lon"),
            P(None, "lat", "lon"),
            P(None, "lat", "lon"),
            P("lat", "lon"),
            P("lon"),
            P(None, ("lon", "lat")),
            P(None, "lat", "lon"),
            P(None, "lat", "lon"),
        ),
        out_specs=P(None, None, "lat", "lon"),
        check_vma=False,
    )
```

```python
import functools

import jax
import jax.numpy as jnp
from jax import lax
from jax.experimental import pallas as pl
from jax.experimental.pallas import tpu as pltpu
from jax.sharding import PartitionSpec as P

H = 8
VMEM = pl.BlockSpec(memory_space=pltpu.VMEM)
SMEM = pl.BlockSpec(memory_space=pltpu.SMEM)
PARAMS = pltpu.CompilerParams(vmem_limit_bytes=20 * 2**20)
F32 = jnp.float32
LANE_GATHER = lax.GatherDimensionNumbers(
    offset_dims=(),
    collapsed_slice_dims=(1,),
    start_index_map=(1,),
    operand_batching_dims=(0,),
    start_indices_batching_dims=(0,),
)


def lane_gather(values, lanes):
    return lax.gather(
        values, lanes[..., None], LANE_GATHER, (1, 1), mode=lax.GatherScatterMode.PROMISE_IN_BOUNDS
    )


def pick_columns(partner, sources):
    lanes = jnp.bitwise_and(partner, 127)
    place = jnp.right_shift(partner, 7)
    result = jnp.zeros((8, 128), F32)
    for tile, rows in sources:
        for half in range(2):
            got = lane_gather(rows[:, 128 * half : 128 * half + 128], lanes)
            result = jnp.where(place == 2 * tile + half, got, result)
    return result


def iota(shape, axis):
    return lax.broadcasted_iota(jnp.int32, shape, axis)


def build_kernel(info, *refs):
    sources, (first, second, fold_rows, slots), held, done = refs[:7], refs[7:11], refs[11:18], refs[18]
    copies = [pltpu.make_async_copy(a, b, done.at[i]) for i, (a, b) in enumerate(zip(sources, held))]
    for copy in copies:
        copy.start()
    for copy in copies:
        copy.wait()
    tracers, east, north, levels, weights, indices, flux = held
    for tracer in range(2):
        for quarter in range(4):
            cut = flux[tracer : tracer + 1, 128 * quarter : 128 * quarter + 128]
            slots[:, 4 * tracer + quarter, :] = jnp.broadcast_to(cut, (128, 128))

    def write(out, rows):
        for tracer in range(2):
            out[16 * tracer : 16 * tracer + 16] = tracers[tracer, :, rows, :]
        out[32:48] = east[:, rows, :]
        out[48:64] = north[:, rows, :]
        out[64:68] = weights[:, rows, :]
        out[68:72] = indices[:, rows, :].astype(F32)
        out[72] = levels[rows, :].astype(F32)

    is_odd = info[6] == 1

    @pl.when(is_odd)
    def _():
        write(first, slice(0, 8))
        write(second, slice(8, 16))

    @pl.when(jnp.logical_not(is_odd))
    def _():
        write(first, slice(8, 16))
        write(second, slice(0, 8))

    for r in range(2):
        for tracer in range(2):
            at = 4 * r + 2 * tracer
            for part in range(2):
                fold_rows[at + part] = tracers[tracer, 8 * part : 8 * part + 8, 15 - r, :]
        wet = levels[15 - r : 16 - r, :] > 0
        for j in range(4):
            weight = weights[j, 15 - r : 16 - r, :]
            fold_rows[8 + r, j : j + 1, :] = jnp.where(wet, weight, jnp.zeros_like(weight))
            fold_rows[8 + r, 4 + j : 5 + j, :] = indices[j, 15 - r : 16 - r, :].astype(F32)

    @pl.when(info[1] == 1)
    def _():
        second[0:10] = fold_rows[...]


class Sides:
    def __init__(self, info, first, second):
        self.odd, self.top = info[6] == 1, info[1] == 1
        self.first, self.second = first, second

    def south(self, plane, cut=slice(None)):
        return jnp.where(self.odd, self.first[plane, :, cut], self.second[plane, :, cut])

    def north(self, plane, cut=slice(None)):
        got = jnp.where(self.odd, self.second[plane, :, cut], self.first[plane, :, cut])
        return jnp.where(self.top, 0.0, got)

    def whole(self, plane, centre, cut=slice(None)):
        return jnp.concatenate([self.south(plane, cut), centre, self.north(plane, cut)], axis=0)


def pack_kernel(info, tracers, east, north, levels, weights, indices, partner, first, second, fold_b, ghosts, to_west, to_east):
    is_top = info[1] == 1
    wanted = jnp.broadcast_to(partner[...], (8, 256))
    for block in range(10):
        rows = pl.ds(8 * block, 8)
        sources = [(info[2], second[block]), (info[3], fold_b[block])]
        for half in range(2):
            cut = slice(128 * half, 128 * half + 128)
            ghosts[rows, cut] = pick_columns(wanted[:, cut], sources)
    lane = iota((32, 128), 1)
    row = iota((32, 128), 0)
    ghost_first = jnp.logical_and(row == 24, is_top)
    ghost_second = jnp.logical_and(row == 25, is_top)
    last_north = jnp.logical_and(row == 23, is_top)
    beyond = jnp.logical_and(row >= 24, is_top)
    west_cut, east_cut = slice(0, 128), slice(128, 256)

    whole = Sides(info, first, second).whole

    def value(plane, cut):
        if plane < 32:
            got = whole(plane, tracers[plane // 16, plane % 16, :, cut], cut)
            got = jnp.where(ghost_first, ghosts[plane : plane + 1, cut], got)
            return jnp.where(ghost_second, ghosts[32 + plane : 33 + plane, cut], got)
        if plane < 48:
            return whole(plane, east[plane - 32, :, cut], cut)
        if plane < 64:
            return jnp.where(last_north, 0.0, whole(plane, north[plane - 48, :, cut], cut))
        if plane < 72:
            centre = weights[plane - 64, :, cut] if plane < 68 else indices[plane - 68, :, cut].astype(F32)
            got = jnp.where(ghost_first, ghosts[plane : plane + 1, cut], whole(plane, centre, cut))
            return jnp.where(ghost_second, ghosts[plane + 8 : plane + 9, cut], got)
        if plane == 72:
            return jnp.where(beyond, 16.0, whole(plane, levels[:, cut].astype(F32), cut))
        return jnp.broadcast_to(partner[:, cut].astype(F32), (32, 128))

    for group in range(5):
        westward = jnp.zeros((32, 128), F32)
        eastward = jnp.zeros((32, 128), F32)
        for slot in range(16 if group < 4 else 10):
            mine = jnp.logical_and(lane >= 8 * slot, lane < 8 * slot + 8)
            plane = 16 * group + slot
            near = value(plane, west_cut)
            far = value(plane, east_cut)
            westward = jnp.where(mine, pltpu.roll(near, 8 * slot, 1) if slot else near, westward)
            eastward = jnp.where(mine, pltpu.roll(far, (8 * slot + 8) % 128, 1) if slot != 15 else far, eastward)
        to_west[group] = westward
        to_east[group] = eastward


def one_hot_lookup(split_table, high, low, count):
    short = lambda v: jnp.broadcast_to(v, (512, count)).astype(jnp.int16)
    matches = lax.broadcasted_iota(jnp.int16, (512, count), 0) == short(high)
    chosen = jnp.where(matches, jnp.bfloat16(1), jnp.bfloat16(0))
    got = jnp.dot(split_table[...], chosen, preferred_element_type=F32)
    lanes = iota((128, count), 0) == low
    first = jnp.sum(jnp.where(lanes, got[:128] + got[128:256], 0.0), axis=0, keepdims=True)
    second = jnp.sum(jnp.where(lanes, got[256:384] + got[384:], 0.0), axis=0, keepdims=True)
    return first, second


def split_place(index):
    high = jnp.bitwise_and(jnp.right_shift(index, 7), 3) * 128 + jnp.right_shift(index, 9)
    return high, jnp.bitwise_and(index, 127)


def split_kernel_table(table, split_table):
    for tracer in range(2):
        for quarter in range(4):
            block = table[:, tracer * 4 + quarter, :].T
            top = block.astype(jnp.bfloat16)
            rest = (block - top.astype(F32)).astype(jnp.bfloat16)
            cut = slice(128 * quarter, 128 * quarter + 128)
            split_table[tracer * 256 : tracer * 256 + 128, cut] = top
            split_table[tracer * 256 + 128 : tracer * 256 + 256, cut] = rest


def halo_tile(from_east, from_west, lane, group, slot):
    shift = (lambda v: v % 128) if isinstance(slot, int) else (lambda v: lax.rem(v, 128))
    near = pltpu.roll(from_east[group], shift(128 - 8 * slot), 1)
    far = pltpu.roll(from_west[group], shift(248 - 8 * slot), 1)
    return jnp.where(lane < 8, near, jnp.where(lane >= 120, far, 0.0))


def lookup_kernel(groups, splits, last, info, table, *rest):
    if splits:
        weights, indices, first, second, ghosts, surface, split_table, high, low, weight = rest
        split_kernel_table(table, split_table)
        is_top = info[1] == 1
        whole = Sides(info, first, second).whole
        row = iota((32, 256), 0)
        for j in range(4):
            index = whole(68 + j, indices[j].astype(F32))
            scale = whole(64 + j, weights[j])
            for r in range(2):
                ghost = jnp.logical_and(row == 24 + r, is_top)
                scale = jnp.where(ghost, ghosts[64 + 8 * r + j : 65 + 8 * r + j, :], scale)
                index = jnp.where(ghost, ghosts[68 + 8 * r + j : 69 + 8 * r + j, :], index)
            high[j], low[j] = split_place(index.astype(jnp.int32))
            weight[j] = scale
    else:
        split_table = table
        if last:
            high, low, weight, from_east, from_west, surface, halo_surface = rest
        else:
            high, low, weight, surface = rest
    for i, group in enumerate(groups):
        totals = [[jnp.zeros((1, 256), F32) for _ in range(4)] for _ in range(2)]
        for j in range(4):
            rows = [slice(4 * group + q, 4 * group + q + 1) for q in range(4)]
            join = lambda ref: jnp.concatenate([ref[j, r, :] for r in rows], axis=1)
            pair = one_hot_lookup(split_table, join(high), join(low), 1024)
            for q, r in enumerate(rows):
                for tracer in range(2):
                    totals[tracer][q] += weight[j, r, :] * pair[tracer][:, 256 * q : 256 * q + 256]
        for tracer in range(2):
            for q in range(4):
                surface[tracer, 4 * i + q : 4 * i + q + 1, :] = totals[tracer][q]
    if last:
        lane = iota((32, 128), 1)
        small_lane, small_row = iota((16, 128), 1), iota((16, 128), 0)
        places, scales = [], []
        for j in range(4):
            index = halo_tile(from_east, from_west, lane, 4, 4 + j)
            scale = halo_tile(from_east, from_west, lane, 4, j)
            for part in range(2):
                cut = slice(16 * part, 16 * part + 16)
                places.append(spread_rows(index[cut], small_row, small_lane).astype(jnp.int32))
                scales.append(spread_rows(scale[cut], small_row, small_lane))
        halo_high, halo_low = split_place(jnp.concatenate(places, axis=1))
        pair = one_hot_lookup(split_table, halo_high, halo_low, 1024)
        for tracer in range(2):
            for part in range(2):
                total = jnp.zeros((1, 128), F32)
                for j in range(4):
                    at = 2 * j + part
                    total += scales[at] * pair[tracer][:, 128 * at : 128 * at + 128]
                halo_surface[tracer, 16 * part : 16 * part + 16, :] = gather_rows(total, small_row, small_lane)


def spread_rows(halo, row_of, lane):
    moved = jnp.where(lane < 8, pltpu.roll(halo, 4, 1), jnp.zeros_like(halo))
    for shift in (8, 16, 32, 64):
        moved = moved + pltpu.roll(moved, shift, 1)
    return jnp.sum(jnp.where(lane // 8 == row_of, moved, jnp.zeros_like(moved)), axis=0, keepdims=True)


def gather_rows(packed, row_of, lane):
    moved = jnp.where(lane // 8 == row_of, jnp.broadcast_to(packed, (16, 128)), 0.0)
    for shift in (8, 16, 32, 64):
        moved = moved + pltpu.roll(moved, shift, 1)
    return pltpu.roll(moved, 124, 1)


def east_of(f):
    return pltpu.roll(f, f.shape[1] - 1, 1)


def west_of(f):
    return pltpu.roll(f, 1, 1)


def north_of(f):
    return pltpu.roll(f, f.shape[0] - 1, 0)


def south_of(f):
    return pltpu.roll(f, 1, 0)


def run_levels(cells, half_east, half_north, depth, surface, store, window=slice(0, 32), keep=slice(0, 32), tracers=(0, 1), unroll=2):
    depth = depth[window, :]
    east_depth = jnp.minimum(depth, east_of(depth))
    north_depth = jnp.minimum(depth, north_of(depth))
    kept = slice(window.start + keep.start, window.start + keep.stop)

    def body(k, carry):
        level = k.astype(F32)
        east_open, north_open, wet = level < east_depth, level < north_depth, level < depth[keep]
        deeper = level + 1.0 < depth[keep]
        east, north = half_east[k, window, :], half_north[k, window, :]
        above, under = jnp.minimum(k + 1, 15), jnp.maximum(k - 1, 0)
        at_surface = jnp.where(k == 0, 0.5, 0.0).astype(F32)
        for tracer in tracers:
            here = cells[tracer, k]
            to_east, to_north = east_of(here), north_of(here)
            grad_east = jnp.where(east_open, to_east - here, 0.0)
            grad_north = jnp.where(north_open, to_north - here, 0.0)
            lap = grad_east - west_of(grad_east) + (grad_north - south_of(grad_north))
            flat = 0.08 * here - 0.01 * lap
            flux_east = jnp.where(east_open, east_of(flat) - flat - east * (to_east + here), 0.0)
            flux_north = jnp.where(north_open, north_of(flat) - flat - north * (to_north + here), 0.0)
            total = (flux_east - west_of(flux_east) + (flux_north - south_of(flux_north)))[keep]
            centre = here[keep]
            vertical = jnp.where(deeper, cells[tracer, above, keep, :] - centre, 0.0)
            total += 0.1 * (vertical - (centre - cells[tracer, under, keep, :]))
            if surface is not None:
                total += at_surface * surface[tracer, kept, :]
            store(tracer, k, centre + jnp.where(wet, total, 0.0))
        return carry

    lax.fori_loop(0, 16, body, 0, unroll=unroll)


def keep_step(cells_out, fold_out):
    def store(tracer, k, fresh):
        cells_out[tracer, k] = fresh
        for r in range(2):
            fold_out[pl.ds(32 * r + 16 * tracer + k, 1), :] = fresh[23 - r : 24 - r, 0:256]

    return store


def place_ghosts(cells, ghosts, columns, row=24):
    def place(k, carry):
        for tracer in range(2):
            for r in range(2):
                cells[tracer, k, row + r : row + r + 1, 0:columns] = ghosts[pl.ds(32 * r + 16 * tracer + k, 1), :]
        return carry

    lax.fori_loop(0, 16, place, 0)


def first_kernel(
    info, tracers, east, north, levels, partner, first, second, ghosts, from_east, from_west,
    cells_out, fold_out, east_ext, north_ext, depth_ext, partner_ext, start,
):
    is_top = info[1] == 1
    lane = iota((32, 128), 1)
    row = iota((32, 256), 0)
    last_north = jnp.logical_and(row == 23, is_top)
    halo = functools.partial(halo_tile, from_east, from_west, lane)

    whole = Sides(info, first, second).whole

    def fill(k, carry):
        for tracer in range(2):
            start[tracer, k, :, 0:256] = whole(tracer * 16 + k, tracers[tracer, k])
            start[tracer, k, :, 256:384] = halo(tracer, k)
        east_ext[k, :, 0:256] = 0.5 * whole(32 + k, east[k])
        east_ext[k, :, 256:384] = 0.5 * halo(2, k)
        north_ext[k, :, 0:256] = jnp.where(last_north, 0.0, 0.5 * whole(48 + k, north[k]))
        north_ext[k, :, 256:384] = 0.5 * halo(3, k)
        return carry

    lax.fori_loop(0, 16, fill, 0)

    @pl.when(is_top)
    def _():
        place_ghosts(start, ghosts, 256)

    depth_ext[:, 0:256] = jnp.where(
        jnp.logical_and(row >= 24, is_top), 16.0, whole(72, levels[...].astype(F32))
    )
    depth_ext[:, 256:384] = halo(4, 8)
    partner_ext[:, 0:256] = jnp.broadcast_to(partner[...], (8, 256))
    partner_ext[:, 256:384] = halo(4, 9)[0:8].astype(jnp.int32)
    run_levels(start, east_ext, north_ext, depth_ext, None, keep_step(cells_out, fold_out))


def fold_ghosts(info, partner_ext, received, ghosts):
    def block_body(block, carry):
        rows = pl.ds(pl.multiple_of(8 * block, 8), 8)
        all_sources = [(info[2 + i], ref[rows, :]) for i, ref in enumerate(received)]
        for part, sources in enumerate((all_sources[:2], all_sources[:2], all_sources)):
            cut = slice(128 * part, 128 * part + 128)
            ghosts[rows, cut] = pick_columns(partner_ext[:, cut], sources)
        return carry

    lax.fori_loop(0, 8, block_body, 0)


def second_kernel(
    info, cells, east_ext, north_ext, depth_ext, partner_ext, fold_a, fold_b, fold_c, fold_d, surface_a, surface_b, surface_c, surface_d,
    surface_e, halo_surface, cells_out, fold_out, surface_ext, ghosts, start,
):
    def fill(k, carry):
        for tracer in range(2):
            start[tracer, k] = cells[tracer, k]
        return carry

    lax.fori_loop(0, 16, fill, 0)

    @pl.when(info[1] == 1)
    def _():
        fold_ghosts(info, partner_ext, (fold_a, fold_b, fold_c, fold_d), ghosts)
        place_ghosts(start, ghosts, 384)

    surface_ext[...] = jnp.zeros((2, 32, 384), F32)
    for tracer in range(2):
        at = 4
        for piece in (surface_a, surface_b, surface_c, surface_d, surface_e):
            surface_ext[tracer, at : at + piece.shape[1], 0:256] = piece[tracer]
            at += piece.shape[1]
        surface_ext[tracer, :, 256:384] = halo_surface[tracer]
        start[tracer, 0] = start[tracer, 0] + jnp.where(depth_ext[...] > 0.0, 0.5 * surface_ext[tracer], 0.0)
    run_levels(start, east_ext, north_ext, depth_ext, surface_ext, keep_step(cells_out, fold_out))


def last_kernel(
    info, cells, east_ext, north_ext, depth_ext, partner_ext, fold_a, fold_b, fold_c, fold_d, surface_ext, result, ghosts, start
):
    def fill(k, carry):
        for tracer in range(2):
            start[tracer, k] = cells[tracer, k]
        return carry

    lax.fori_loop(0, 16, fill, 0)

    @pl.when(info[1] == 1)
    def _():
        fold_ghosts(info, partner_ext, (fold_a, fold_b, fold_c, fold_d), ghosts)
        place_ghosts(start, ghosts, 384)

    def store(tracer, k, fresh):
        result[tracer, k] = fresh[:, 0:256]

    run_levels(start, east_ext, north_ext, depth_ext, surface_ext, store, keep=slice(8, 24), unroll=4)


def call(kernel, ins, outs, scratch=(), cost=None, earlier=(), ins_any=False, outs_any=False, alias=None, params=PARAMS):
    used = len(ins)

    def body(*refs):
        kernel(*refs[:used], *refs[used + len(earlier) :])

    anywhere = pl.BlockSpec(memory_space=pl.ANY)
    hbm = pl.BlockSpec(memory_space=pltpu.HBM)

    def place(i, v):
        if v.ndim == 1:
            return SMEM
        return hbm if ins_any or i == alias else anywhere if i >= used else VMEM

    arrays = tuple(ins) + tuple(earlier)
    return pl.pallas_call(
        body,
        out_shape=tuple(jax.ShapeDtypeStruct(s, d) for s, d in outs),
        in_specs=[place(i, v) for i, v in enumerate(arrays)],
        out_specs=tuple(hbm if outs_any else VMEM for _ in outs),
        scratch_shapes=list(scratch),
        compiler_params=params,
        cost_estimate=cost,
        input_output_aliases={} if alias is None else {alias: 0},
    )(*arrays)


STEP_COST = pl.CostEstimate(flops=10**7, bytes_accessed=16 * 2**20, transcendentals=0)


def lookup_cost(groups):
    return pl.CostEstimate(flops=groups * 2 * 512 * 512 * 4096, bytes_accessed=groups * 2**20, transcendentals=0)


def per_device(tracers, east, north, levels, partner, atm_flux, indices, weights):
    nlon, nlat = lax.axis_size("lon"), lax.axis_size("lat")
    both = ("lon", "lat")
    t, lat = lax.axis_index("lon"), lax.axis_index("lat")
    is_top = (lat == nlat - 1).astype(jnp.int32)
    tiles = [jnp.remainder(nlon - 1 - t + d, nlon) for d in (0, 1, -1, 2)]
    info = jnp.stack([t, is_top] + tiles + [lat % 2]).astype(jnp.int32)
    top = nlat - 1

    def fold_permute(rows, d):
        pairs = [(i * nlat + top, ((nlon - 1 + d - i) % nlon) * nlat + top) for i in range(nlon)]
        return lax.ppermute(rows, both, pairs)

    message = ((73, H, 256), F32)
    whole_inputs = (tracers, east, north, levels, weights, indices)
    build_inputs = (*whole_inputs, atm_flux)
    first, second, fold_rows, slots = call(
        build_kernel,
        (info, *build_inputs),
        [message, message, ((10, 8, 256), F32), ((nlon * nlat, 8, 128), F32)],
        [pltpu.VMEM(a.shape, a.dtype) for a in build_inputs] + [pltpu.SemaphoreType.DMA((7,))],
        ins_any=True,
        params=pltpu.CompilerParams(vmem_limit_bytes=60 * 2**20),
    )
    def after(value, *earlier):
        return lax.optimization_barrier((value, *earlier))[0]

    swaps = [(i, i + 1) for i in range(0, nlat, 2)]
    first = lax.ppermute(first, "lat", swaps + [(j, i) for i, j in swaps])
    swaps = [(i, i + 1) for i in range(1, nlat - 1, 2)]
    swaps = [(c * nlat + i, c * nlat + j) for c in range(nlon) for i, j in swaps + [(j, i) for i, j in swaps]]
    facing = [(c * nlat + top, (nlon - 1 - c) * nlat + top) for c in range(nlon)]
    second = lax.ppermute(second, both, swaps + facing)
    fold_b = fold_permute(fold_rows, 1)

    table = lax.all_to_all(slots, both, 0, 0, tiled=True)

    partner_row = partner.reshape(1, -1)
    ghosts, to_west, to_east = call(
        pack_kernel,
        (info, *whole_inputs, partner_row, first, second, fold_b),
        [((80, 256), F32), ((5, 32, 128), F32), ((5, 32, 128), F32)],
    )
    from_east = lax.ppermute(to_west, "lon", [((i + 1) % nlon, i) for i in range(nlon)])
    from_west = lax.ppermute(to_east, "lon", [(i, (i + 1) % nlon) for i in range(nlon)])

    def lookups(groups, ins, splits=False, last=False, earlier=()):
        outs = [((2, 4 * len(groups), 256), F32)]
        places = ((4, 32, 256), jnp.int32)
        outs += [((512, 512), jnp.bfloat16), places, places, (places[0], F32)] if splits else []
        outs += [((2, 32, 128), F32)] if last else []
        return call(
            functools.partial(lookup_kernel, groups, splits, last), (info, *ins), outs, (), lookup_cost(len(groups)), earlier
        )

    surface_a, *places = lookups((1, 2), (table, weights, indices, first, second, ghosts), splits=True)

    wide = (2, 16, 32, 384)
    cells, fold_rows, east_ext, north_ext, depth_ext, partner_ext = call(
        first_kernel,
        (info, tracers, east, north, levels, partner_row, first, second, ghosts, from_east, from_west),
        [(wide, F32), ((64, 256), F32), (wide[1:], F32), (wide[1:], F32), ((32, 384), F32), ((8, 384), jnp.int32)],
        [pltpu.VMEM(wide, F32)],
        STEP_COST,
        (surface_a,),
    )
    statics = (east_ext, north_ext, depth_ext)
    received = [fold_permute(fold_rows, 0)]
    (surface_b,) = lookups((3,), places, earlier=(fold_rows,))
    received.append(fold_permute(after(fold_rows, surface_b), 1))
    (surface_c,) = lookups((4,), places, earlier=(received[0], surface_b))
    received.append(fold_permute(after(fold_rows, surface_c), -1))
    (surface_d,) = lookups((5,), places, earlier=(received[1], surface_c))
    received.append(fold_permute(after(fold_rows, surface_d), 2))
    surface_e, halo_surface = lookups((6,), (*places, from_east, from_west), last=True, earlier=(received[2], surface_d))

    ghost_rows = pltpu.VMEM((64, 384), F32)
    cells, fold_rows, surface_ext = call(
        second_kernel,
        (info, cells, *statics, partner_ext, *received, surface_a, surface_b, surface_c, surface_d, surface_e,
         halo_surface),
        [(wide, F32), ((64, 256), F32), ((2, 32, 384), F32)],
        [ghost_rows, pltpu.VMEM(wide, F32)],
        STEP_COST,
    )
    received = [fold_permute(fold_rows, d) for d in (0, 1, -1, 2)]
    (result,) = call(
        last_kernel,
        (info, cells, *statics, partner_ext, *received, surface_ext),
        [(tracers.shape, F32)],
        [ghost_rows, pltpu.VMEM(wide, F32)],
        STEP_COST,
    )
    return result


def solution(mesh):
    return jax.shard_map(
        per_device,
        mesh=mesh,
        in_specs=(
            P(None, None, "lat", "lon"),
            P(None, "lat", "lon"),
            P(None, "lat", "lon"),
            P("lat", "lon"),
            P("lon"),
            P(None, ("lon", "lat")),
            P(None, "lat", "lon"),
            P(None, "lat", "lon"),
        ),
        out_specs=P(None, None, "lat", "lon"),
        check_vma=False,
    )
```

```python
import functools

import jax
import jax.numpy as jnp
from jax import lax
from jax.experimental import pallas as pl
from jax.experimental.pallas import tpu as pltpu
from jax.sharding import PartitionSpec as P

H = 8
PLANES = 64
VMEM = pl.BlockSpec(memory_space=pltpu.VMEM)
PARAMS = pltpu.CompilerParams(vmem_limit_bytes=20 * 2**20)
F32 = jnp.float32
LANE_GATHER = lax.GatherDimensionNumbers(
    offset_dims=(),
    collapsed_slice_dims=(1,),
    start_index_map=(1,),
    operand_batching_dims=(0,),
    start_indices_batching_dims=(0,),
)


def lane_gather(values, lanes):
    return lax.gather(
        values, lanes[..., None], LANE_GATHER, (1, 1), mode=lax.GatherScatterMode.PROMISE_IN_BOUNDS
    )


def own_place():
    nlon, nlat = lax.axis_size("lon"), lax.axis_size("lat")
    t, lat = lax.axis_index("lon"), lax.axis_index("lat")
    tiles = [lax.rem(2 * nlon - 1 - t + d, nlon) for d in (0, 1, -1, 2)]
    return [t, (lat == nlat - 1).astype(jnp.int32), *tiles, lax.rem(lat, 2)]


def pick_columns(partner, sources):
    lanes = jnp.bitwise_and(partner, 127)
    place = jnp.right_shift(partner, 7)
    result = jnp.zeros((8, 128), F32)
    for tile, rows in sources:
        for half in range(2):
            got = lane_gather(rows[:, 128 * half : 128 * half + 128], lanes)
            result = jnp.where(place == 2 * tile + half, got, result)
    return result


def iota(shape, axis):
    return lax.broadcasted_iota(jnp.int32, shape, axis)


def build_kernel(info, *refs):
    sources, (first, second, fold_rows, slots), held, done = refs[:7], refs[7:11], refs[11:18], refs[18]
    copies = [pltpu.make_async_copy(a, b, done.at[i]) for i, (a, b) in enumerate(zip(sources, held))]
    for copy in copies:
        copy.start()
    for copy in copies:
        copy.wait()
    tracers, east, north, levels, weights, indices, flux = held
    for tracer in range(2):
        for quarter in range(4):
            cut = flux[tracer : tracer + 1, 128 * quarter : 128 * quarter + 128]
            slots[:, 4 * tracer + quarter, :] = jnp.broadcast_to(cut, (128, 128))

    def write(out, rows, near, fifth):
        for tracer in range(2):
            out[16 * tracer : 16 * tracer + 16] = tracers[tracer, :, rows, :]
        for half in range(2):
            levels_in, rows_out = slice(8 * half, 8 * half + 8), slice(4 * half, 4 * half + 4)
            out[32:40, rows_out, :] = east[levels_in, near, :]
            out[40:48, rows_out, :] = north[levels_in, near, :]
            out[53 + half] = north[levels_in, fifth, :]
        out[48:52, 0:4, :] = weights[:, near, :]
        out[48:52, 4:8, :] = indices[:, near, :].astype(F32)
        out[52] = levels[rows, :].astype(F32)
        out[55:PLANES] = jnp.zeros((PLANES - 55, H, 256), F32)

    southward, northward = (slice(0, 8), slice(0, 4), 4), (slice(8, 16), slice(12, 16), 11)
    is_odd = info[6] == 1

    @pl.when(is_odd)
    def _():
        write(first, *southward)
        write(second, *northward)

    @pl.when(jnp.logical_not(is_odd))
    def _():
        write(first, *northward)
        write(second, *southward)

    for r in range(2):
        for tracer in range(2):
            at = 4 * r + 2 * tracer
            for part in range(2):
                fold_rows[at + part] = tracers[tracer, 8 * part : 8 * part + 8, 15 - r, :]
        wet = levels[15 - r : 16 - r, :] > 0
        for j in range(4):
            weight = weights[j, 15 - r : 16 - r, :]
            fold_rows[8 + r, j : j + 1, :] = jnp.where(wet, weight, jnp.zeros_like(weight))
            fold_rows[8 + r, 4 + j : 5 + j, :] = indices[j, 15 - r : 16 - r, :].astype(F32)

    @pl.when(info[1] == 1)
    def _():
        second[0:10] = fold_rows[...]


class Sides:
    def __init__(self, info, first, second):
        self.odd, self.top = info[6] == 1, info[1] == 1
        self.first, self.second = first, second

    def blocks(self, plane, cut):
        first, second = self.first[plane, :, cut], self.second[plane, :, cut]
        north = jnp.where(self.top, 0.0, jnp.where(self.odd, second, first))
        return jnp.where(self.odd, first, second), north

    def whole(self, plane, centre, cut=slice(None)):
        south, north = self.blocks(plane, cut)
        return jnp.concatenate([south, centre, north], axis=0)

    def near(self, plane, upper, centre, cut=slice(None)):
        south, north = self.blocks(plane, cut)
        turned_south, turned_north = pltpu.roll(south, 4, 0), pltpu.roll(north, 4, 0)
        if isinstance(upper, bool):
            south, north = (south, turned_north) if upper else (turned_south, north)
        else:
            south, north = jnp.where(upper, south, turned_south), jnp.where(upper, turned_north, north)
        return jnp.concatenate([south, centre, north], axis=0)

    def velocity(self, first_plane, k, centre, cut=slice(None)):
        if isinstance(k, int):
            return self.near(first_plane + k % 8, k >= 8, centre, cut)
        return self.near(first_plane + jnp.bitwise_and(k, 7), k >= 8, centre, cut)

    def north_velocity(self, k, centre, cut=slice(None)):
        got = self.velocity(40, k, centre, cut)
        plane, at = (53 + k // 8, k % 8) if isinstance(k, int) else (53 + jnp.right_shift(k, 3), jnp.bitwise_and(k, 7))
        row = pl.ds(at, 1)
        fifth = jnp.where(self.odd, self.first[plane, row, cut], self.second[plane, row, cut])
        return jnp.where(iota(got.shape, 0) == 3, fifth, got)


def pack_kernel(info, tracers, east, north, levels, weights, indices, partner, first, second, fold_b, ghosts, to_west, to_east):
    is_top = info[1] == 1
    wanted = jnp.broadcast_to(partner[...], (8, 256))
    for block in range(10):
        rows = pl.ds(8 * block, 8)
        sources = [(info[2], second[block]), (info[3], fold_b[block])]
        for half in range(2):
            cut = slice(128 * half, 128 * half + 128)
            ghosts[rows, cut] = pick_columns(wanted[:, cut], sources)
    lane = iota((32, 128), 1)
    row = iota((32, 128), 0)
    ghost_first = jnp.logical_and(row == 24, is_top)
    ghost_second = jnp.logical_and(row == 25, is_top)
    last_north = jnp.logical_and(row == 23, is_top)
    beyond = jnp.logical_and(row >= 24, is_top)
    west_cut, east_cut = slice(0, 128), slice(128, 256)

    sides = Sides(info, first, second)
    whole = sides.whole

    def value(plane, cut):
        if plane < 32:
            got = whole(plane, tracers[plane // 16, plane % 16, :, cut], cut)
            got = jnp.where(ghost_first, ghosts[plane : plane + 1, cut], got)
            return jnp.where(ghost_second, ghosts[32 + plane : 33 + plane, cut], got)
        if plane < 48:
            return sides.velocity(32, plane - 32, east[plane - 32, :, cut], cut)
        if plane < 64:
            return jnp.where(last_north, 0.0, sides.north_velocity(plane - 48, north[plane - 48, :, cut], cut))
        if plane < 72:
            centre = weights[plane - 64, :, cut] if plane < 68 else indices[plane - 68, :, cut].astype(F32)
            got = sides.near(48 + plane % 4, plane >= 68, centre, cut)
            got = jnp.where(ghost_first, ghosts[plane : plane + 1, cut], got)
            return jnp.where(ghost_second, ghosts[plane + 8 : plane + 9, cut], got)
        if plane == 72:
            return jnp.where(beyond, 16.0, whole(52, levels[:, cut].astype(F32), cut))
        return jnp.broadcast_to(partner[:, cut].astype(F32), (32, 128))

    for group in range(5):
        westward = jnp.zeros((32, 128), F32)
        eastward = jnp.zeros((32, 128), F32)
        for slot in range(16 if group < 4 else 10):
            mine = jnp.logical_and(lane >= 8 * slot, lane < 8 * slot + 8)
            plane = 16 * group + slot
            near = value(plane, west_cut)
            far = value(plane, east_cut)
            westward = jnp.where(mine, pltpu.roll(near, 8 * slot, 1) if slot else near, westward)
            eastward = jnp.where(mine, pltpu.roll(far, (8 * slot + 8) % 128, 1) if slot != 15 else far, eastward)
        to_west[group] = westward
        to_east[group] = eastward


def one_hot_lookup(split_table, high, low, count):
    short = lambda v: jnp.broadcast_to(v, (512, count)).astype(jnp.int16)
    matches = lax.broadcasted_iota(jnp.int16, (512, count), 0) == short(high)
    chosen = jnp.where(matches, jnp.bfloat16(1), jnp.bfloat16(0))
    got = jnp.dot(split_table[...], chosen, preferred_element_type=F32)
    lanes = iota((128, count), 0) == low
    first = jnp.sum(jnp.where(lanes, got[:128] + got[128:256], 0.0), axis=0, keepdims=True)
    second = jnp.sum(jnp.where(lanes, got[256:384] + got[384:], 0.0), axis=0, keepdims=True)
    return first, second


def split_place(index):
    high = jnp.bitwise_and(jnp.right_shift(index, 7), 3) * 128 + jnp.right_shift(index, 9)
    return high, jnp.bitwise_and(index, 127)


def split_kernel_table(table, split_table):
    for tracer in range(2):
        for quarter in range(4):
            block = table[:, tracer * 4 + quarter, :].T
            top = block.astype(jnp.bfloat16)
            rest = (block - top.astype(F32)).astype(jnp.bfloat16)
            cut = slice(128 * quarter, 128 * quarter + 128)
            split_table[tracer * 256 : tracer * 256 + 128, cut] = top
            split_table[tracer * 256 + 128 : tracer * 256 + 256, cut] = rest


def halo_tile(from_east, from_west, lane, group, slot):
    shift = (lambda v: v % 128) if isinstance(slot, int) else (lambda v: lax.rem(v, 128))
    near = pltpu.roll(from_east[group], shift(128 - 8 * slot), 1)
    far = pltpu.roll(from_west[group], shift(248 - 8 * slot), 1)
    return jnp.where(lane < 8, near, jnp.where(lane >= 120, far, 0.0))


def lookup_kernel(groups, splits, last, info, table, *rest):
    if splits:
        weights, indices, first, second, ghosts, surface, split_table, high, low, weight = rest
        split_kernel_table(table, split_table)
        is_top = info[1] == 1
        near = Sides(info, first, second).near
        row = iota((32, 256), 0)
        for j in range(4):
            index = near(48 + j, True, indices[j].astype(F32))
            scale = near(48 + j, False, weights[j])
            for r in range(2):
                ghost = jnp.logical_and(row == 24 + r, is_top)
                scale = jnp.where(ghost, ghosts[64 + 8 * r + j : 65 + 8 * r + j, :], scale)
                index = jnp.where(ghost, ghosts[68 + 8 * r + j : 69 + 8 * r + j, :], index)
            high[j], low[j] = split_place(index.astype(jnp.int32))
            weight[j] = scale
    else:
        split_table = table
        if last:
            high, low, weight, from_east, from_west, surface, halo_surface = rest
        else:
            high, low, weight, surface = rest
    for i, group in enumerate(groups):
        totals = [[jnp.zeros((1, 256), F32) for _ in range(4)] for _ in range(2)]
        for j in range(4):
            rows = [slice(4 * group + q, 4 * group + q + 1) for q in range(4)]
            join = lambda ref: jnp.concatenate([ref[j, r, :] for r in rows], axis=1)
            pair = one_hot_lookup(split_table, join(high), join(low), 1024)
            for q, r in enumerate(rows):
                for tracer in range(2):
                    totals[tracer][q] += weight[j, r, :] * pair[tracer][:, 256 * q : 256 * q + 256]
        for tracer in range(2):
            for q in range(4):
                surface[tracer, 4 * i + q : 4 * i + q + 1, :] = totals[tracer][q]
    if last:
        lane = iota((32, 128), 1)
        small_lane, small_row = iota((16, 128), 1), iota((16, 128), 0)
        places, scales = [], []
        for j in range(4):
            index = halo_tile(from_east, from_west, lane, 4, 4 + j)
            scale = halo_tile(from_east, from_west, lane, 4, j)
            for part in range(2):
                cut = slice(16 * part, 16 * part + 16)
                places.append(spread_rows(index[cut], small_row, small_lane).astype(jnp.int32))
                scales.append(spread_rows(scale[cut], small_row, small_lane))
        halo_high, halo_low = split_place(jnp.concatenate(places, axis=1))
        pair = one_hot_lookup(split_table, halo_high, halo_low, 1024)
        for tracer in range(2):
            for part in range(2):
                total = jnp.zeros((1, 128), F32)
                for j in range(4):
                    at = 2 * j + part
                    total += scales[at] * pair[tracer][:, 128 * at : 128 * at + 128]
                halo_surface[tracer, 16 * part : 16 * part + 16, :] = gather_rows(total, small_row, small_lane)


def spread_rows(halo, row_of, lane):
    moved = jnp.where(lane < 8, pltpu.roll(halo, 4, 1), jnp.zeros_like(halo))
    for shift in (8, 16, 32, 64):
        moved = moved + pltpu.roll(moved, shift, 1)
    return jnp.sum(jnp.where(lane // 8 == row_of, moved, jnp.zeros_like(moved)), axis=0, keepdims=True)


def gather_rows(packed, row_of, lane):
    moved = jnp.where(lane // 8 == row_of, jnp.broadcast_to(packed, (16, 128)), 0.0)
    for shift in (8, 16, 32, 64):
        moved = moved + pltpu.roll(moved, shift, 1)
    return pltpu.roll(moved, 124, 1)


def east_of(f):
    return pltpu.roll(f, f.shape[1] - 1, 1)


def west_of(f):
    return pltpu.roll(f, 1, 1)


def north_of(f):
    return pltpu.roll(f, f.shape[0] - 1, 0)


def south_of(f):
    return pltpu.roll(f, 1, 0)


def run_levels(cells, half_east, half_north, depth, surface, store, window=slice(0, 32), keep=slice(0, 32), tracers=(0, 1), unroll=2):
    depth = depth[window, :]
    east_depth = jnp.minimum(depth, east_of(depth))
    north_depth = jnp.minimum(depth, north_of(depth))
    kept = slice(window.start + keep.start, window.start + keep.stop)

    def body(k, carry):
        level = k.astype(F32)
        east_open, north_open, wet = level < east_depth, level < north_depth, level < depth[keep]
        deeper = level + 1.0 < depth[keep]
        east, north = half_east[k, window, :], half_north[k, window, :]
        above, under = jnp.minimum(k + 1, 15), jnp.maximum(k - 1, 0)
        at_surface = jnp.where(k == 0, 0.5, 0.0).astype(F32)
        for tracer in tracers:
            here = cells[tracer, k]
            to_east, to_north = east_of(here), north_of(here)
            grad_east = jnp.where(east_open, to_east - here, 0.0)
            grad_north = jnp.where(north_open, to_north - here, 0.0)
            lap = grad_east - west_of(grad_east) + (grad_north - south_of(grad_north))
            flat = 0.08 * here - 0.01 * lap
            flux_east = jnp.where(east_open, east_of(flat) - flat - east * (to_east + here), 0.0)
            flux_north = jnp.where(north_open, north_of(flat) - flat - north * (to_north + here), 0.0)
            total = (flux_east - west_of(flux_east) + (flux_north - south_of(flux_north)))[keep]
            centre = here[keep]
            vertical = jnp.where(deeper, cells[tracer, above, keep, :] - centre, 0.0)
            total += 0.1 * (vertical - (centre - cells[tracer, under, keep, :]))
            if surface is not None:
                total += at_surface * surface[tracer, kept, :]
            store(tracer, k, centre + jnp.where(wet, total, 0.0))
        return carry

    lax.fori_loop(0, 16, body, 0, unroll=unroll)


def keep_step(cells_out, fold_out):
    def store(tracer, k, fresh):
        cells_out[tracer, k] = fresh
        for r in range(2):
            fold_out[pl.ds(32 * r + 16 * tracer + k, 1), :] = fresh[23 - r : 24 - r, 0:256]

    return store


def place_ghosts(cells, ghosts, columns, row=24):
    def place(k, carry):
        for tracer in range(2):
            for r in range(2):
                cells[tracer, k, row + r : row + r + 1, 0:columns] = ghosts[pl.ds(32 * r + 16 * tracer + k, 1), :]
        return carry

    lax.fori_loop(0, 16, place, 0)


def first_kernel(
    info, tracers, east, north, levels, partner, first, second, ghosts, from_east, from_west,
    cells_out, fold_out, east_ext, north_ext, depth_ext, partner_ext, start,
):
    is_top = info[1] == 1
    lane = iota((32, 128), 1)
    row = iota((32, 256), 0)
    last_north = jnp.logical_and(row == 23, is_top)
    halo = functools.partial(halo_tile, from_east, from_west, lane)

    sides = Sides(info, first, second)
    whole = sides.whole

    def fill(k, carry):
        for tracer in range(2):
            start[tracer, k, :, 0:256] = whole(tracer * 16 + k, tracers[tracer, k])
            start[tracer, k, :, 256:384] = halo(tracer, k)
        east_ext[k, :, 0:256] = 0.5 * sides.velocity(32, k, east[k])
        east_ext[k, :, 256:384] = 0.5 * halo(2, k)
        north_ext[k, :, 0:256] = jnp.where(last_north, 0.0, 0.5 * sides.north_velocity(k, north[k]))
        north_ext[k, :, 256:384] = 0.5 * halo(3, k)
        return carry

    lax.fori_loop(0, 16, fill, 0)

    @pl.when(is_top)
    def _():
        place_ghosts(start, ghosts, 256)

    depth_ext[:, 0:256] = jnp.where(
        jnp.logical_and(row >= 24, is_top), 16.0, whole(52, levels[...].astype(F32))
    )
    depth_ext[:, 256:384] = halo(4, 8)
    partner_ext[:, 0:256] = jnp.broadcast_to(partner[...], (8, 256))
    partner_ext[:, 256:384] = halo(4, 9)[0:8].astype(jnp.int32)
    run_levels(start, east_ext, north_ext, depth_ext, None, keep_step(cells_out, fold_out))


def fold_ghosts(info, partner_ext, received, ghosts):
    def block_body(block, carry):
        rows = pl.ds(pl.multiple_of(8 * block, 8), 8)
        all_sources = [(info[2 + i], ref[rows, :]) for i, ref in enumerate(received)]
        for part, sources in enumerate((all_sources[:2], all_sources[:2], all_sources)):
            cut = slice(128 * part, 128 * part + 128)
            ghosts[rows, cut] = pick_columns(partner_ext[:, cut], sources)
        return carry

    lax.fori_loop(0, 8, block_body, 0)


def second_kernel(
    info, cells, east_ext, north_ext, depth_ext, partner_ext, fold_a, fold_b, fold_c, fold_d, surface_a, surface_b, surface_c, surface_d,
    surface_e, halo_surface, cells_out, fold_out, surface_ext, ghosts, start,
):
    def fill(k, carry):
        for tracer in range(2):
            start[tracer, k] = cells[tracer, k]
        return carry

    lax.fori_loop(0, 16, fill, 0)

    @pl.when(info[1] == 1)
    def _():
        fold_ghosts(info, partner_ext, (fold_a, fold_b, fold_c, fold_d), ghosts)
        place_ghosts(start, ghosts, 384)

    surface_ext[...] = jnp.zeros((2, 32, 384), F32)
    for tracer in range(2):
        at = 4
        for piece in (surface_a, surface_b, surface_c, surface_d, surface_e):
            surface_ext[tracer, at : at + piece.shape[1], 0:256] = piece[tracer]
            at += piece.shape[1]
        surface_ext[tracer, :, 256:384] = halo_surface[tracer]
        start[tracer, 0] = start[tracer, 0] + jnp.where(depth_ext[...] > 0.0, 0.5 * surface_ext[tracer], 0.0)
    run_levels(start, east_ext, north_ext, depth_ext, surface_ext, keep_step(cells_out, fold_out))


def last_kernel(
    info, cells, east_ext, north_ext, depth_ext, partner_ext, fold_a, fold_b, fold_c, fold_d, surface_ext, result, ghosts, start
):
    def fill(k, carry):
        for tracer in range(2):
            start[tracer, k] = cells[tracer, k]
        return carry

    lax.fori_loop(0, 16, fill, 0)

    @pl.when(info[1] == 1)
    def _():
        fold_ghosts(info, partner_ext, (fold_a, fold_b, fold_c, fold_d), ghosts)
        place_ghosts(start, ghosts, 384)

    def store(tracer, k, fresh):
        result[tracer, k] = fresh[:, 0:256]

    run_levels(start, east_ext, north_ext, depth_ext, surface_ext, store, keep=slice(8, 24), unroll=4)


def call(kernel, ins, outs, scratch=(), cost=None, earlier=(), ins_any=False, outs_any=False, alias=None, params=PARAMS):
    used = len(ins)

    def body(*refs):
        kernel(own_place(), *refs[:used], *refs[used + len(earlier) :])

    anywhere = pl.BlockSpec(memory_space=pl.ANY)
    hbm = pl.BlockSpec(memory_space=pltpu.HBM)

    def place(i, v):
        return hbm if ins_any or i == alias else anywhere if i >= used else VMEM

    arrays = tuple(ins) + tuple(earlier)
    return pl.pallas_call(
        body,
        out_shape=tuple(jax.ShapeDtypeStruct(s, d) for s, d in outs),
        in_specs=[place(i, v) for i, v in enumerate(arrays)],
        out_specs=tuple(hbm if outs_any else VMEM for _ in outs),
        scratch_shapes=list(scratch),
        compiler_params=params,
        cost_estimate=cost,
        input_output_aliases={} if alias is None else {alias: 0},
    )(*arrays)


STEP_COST = pl.CostEstimate(flops=10**7, bytes_accessed=16 * 2**20, transcendentals=0)


def lookup_cost(groups):
    return pl.CostEstimate(flops=groups * 2 * 512 * 512 * 4096, bytes_accessed=groups * 2**20, transcendentals=0)


def per_device(tracers, east, north, levels, partner, atm_flux, indices, weights):
    nlon, nlat = lax.axis_size("lon"), lax.axis_size("lat")
    both = ("lon", "lat")
    top = nlat - 1

    def fold_permute(rows, d):
        pairs = [(i * nlat + top, ((nlon - 1 + d - i) % nlon) * nlat + top) for i in range(nlon)]
        return lax.ppermute(rows, both, pairs)

    message = ((PLANES, H, 256), F32)
    whole_inputs = (tracers, east, north, levels, weights, indices)
    build_inputs = (*whole_inputs, atm_flux)
    first, second, fold_rows, slots = call(
        build_kernel,
        build_inputs,
        [message, message, ((10, 8, 256), F32), ((nlon * nlat, 8, 128), F32)],
        [pltpu.VMEM(a.shape, a.dtype) for a in build_inputs] + [pltpu.SemaphoreType.DMA((7,))],
        ins_any=True,
        params=pltpu.CompilerParams(vmem_limit_bytes=60 * 2**20),
    )
    def after(value, *earlier):
        return lax.optimization_barrier((value, *earlier))[0]

    swaps = [(i, i + 1) for i in range(0, nlat, 2)]
    first = lax.ppermute(first, "lat", swaps + [(j, i) for i, j in swaps])
    swaps = [(i, i + 1) for i in range(1, nlat - 1, 2)]
    swaps = [(c * nlat + i, c * nlat + j) for c in range(nlon) for i, j in swaps + [(j, i) for i, j in swaps]]
    facing = [(c * nlat + top, (nlon - 1 - c) * nlat + top) for c in range(nlon)]
    second = lax.ppermute(second, both, swaps + facing)
    fold_b = fold_permute(fold_rows, 1)

    table = lax.all_to_all(slots, both, 0, 0, tiled=True)

    partner_row = partner.reshape(1, -1)
    ghosts, to_west, to_east = call(
        pack_kernel,
        (*whole_inputs, partner_row, first, second, fold_b),
        [((80, 256), F32), ((5, 32, 128), F32), ((5, 32, 128), F32)],
    )
    from_east = lax.ppermute(to_west, "lon", [((i + 1) % nlon, i) for i in range(nlon)])
    from_west = lax.ppermute(to_east, "lon", [(i, (i + 1) % nlon) for i in range(nlon)])

    def lookups(groups, ins, splits=False, last=False, earlier=()):
        outs = [((2, 4 * len(groups), 256), F32)]
        places = ((4, 32, 256), jnp.int32)
        outs += [((512, 512), jnp.bfloat16), places, places, (places[0], F32)] if splits else []
        outs += [((2, 32, 128), F32)] if last else []
        return call(
            functools.partial(lookup_kernel, groups, splits, last), ins, outs, (), lookup_cost(len(groups)), earlier
        )

    surface_a, *places = lookups((1, 2), (table, weights, indices, first, second, ghosts), splits=True)

    wide = (2, 16, 32, 384)
    cells, fold_rows, east_ext, north_ext, depth_ext, partner_ext = call(
        first_kernel,
        (tracers, east, north, levels, partner_row, first, second, ghosts, from_east, from_west),
        [(wide, F32), ((64, 256), F32), (wide[1:], F32), (wide[1:], F32), ((32, 384), F32), ((8, 384), jnp.int32)],
        [pltpu.VMEM(wide, F32)],
        STEP_COST,
        (surface_a,),
    )
    statics = (east_ext, north_ext, depth_ext)
    received = [fold_permute(fold_rows, 0)]
    (surface_b,) = lookups((3,), places, earlier=(fold_rows,))
    received.append(fold_permute(after(fold_rows, surface_b), 1))
    (surface_c,) = lookups((4,), places, earlier=(received[0], surface_b))
    received.append(fold_permute(after(fold_rows, surface_c), -1))
    (surface_d,) = lookups((5,), places, earlier=(received[1], surface_c))
    received.append(fold_permute(after(fold_rows, surface_d), 2))
    surface_e, halo_surface = lookups((6,), (*places, from_east, from_west), last=True, earlier=(received[2], surface_d))

    ghost_rows = pltpu.VMEM((64, 384), F32)
    cells, fold_rows, surface_ext = call(
        second_kernel,
        (cells, *statics, partner_ext, *received, surface_a, surface_b, surface_c, surface_d, surface_e,
         halo_surface),
        [(wide, F32), ((64, 256), F32), ((2, 32, 384), F32)],
        [ghost_rows, pltpu.VMEM(wide, F32)],
        STEP_COST,
    )
    received = [fold_permute(fold_rows, d) for d in (0, 1, -1, 2)]
    (result,) = call(
        last_kernel,
        (cells, *statics, partner_ext, *received, surface_ext),
        [(tracers.shape, F32)],
        [ghost_rows, pltpu.VMEM(wide, F32)],
        STEP_COST,
    )
    return result


def solution(mesh):
    return jax.shard_map(
        per_device,
        mesh=mesh,
        in_specs=(
            P(None, None, "lat", "lon"),
            P(None, "lat", "lon"),
            P(None, "lat", "lon"),
            P("lat", "lon"),
            P("lon"),
            P(None, ("lon", "lat")),
            P(None, "lat", "lon"),
            P(None, "lat", "lon"),
        ),
        out_specs=P(None, None, "lat", "lon"),
        check_vma=False,
    )
```

```python
import functools

import jax
import jax.numpy as jnp
from jax import lax
from jax.experimental import pallas as pl
from jax.experimental.pallas import tpu as pltpu
from jax.sharding import PartitionSpec as P

H = 8
PLANES = 64
VMEM = pl.BlockSpec(memory_space=pltpu.VMEM)
PARAMS = pltpu.CompilerParams(vmem_limit_bytes=20 * 2**20)
F32 = jnp.float32
LANE_GATHER = lax.GatherDimensionNumbers(
    offset_dims=(),
    collapsed_slice_dims=(1,),
    start_index_map=(1,),
    operand_batching_dims=(0,),
    start_indices_batching_dims=(0,),
)


def lane_gather(values, lanes):
    return lax.gather(
        values, lanes[..., None], LANE_GATHER, (1, 1), mode=lax.GatherScatterMode.PROMISE_IN_BOUNDS
    )


def own_place():
    nlon, nlat = lax.axis_size("lon"), lax.axis_size("lat")
    t, lat = lax.axis_index("lon"), lax.axis_index("lat")
    tiles = [lax.rem(2 * nlon - 1 - t + d, nlon) for d in (0, 1, -1, 2)]
    return [t, (lat == nlat - 1).astype(jnp.int32), *tiles, lax.rem(lat, 2)]


def pick_columns(partner, sources):
    lanes = jnp.bitwise_and(partner, 127)
    place = jnp.right_shift(partner, 7)
    result = jnp.zeros((8, 128), F32)
    for tile, rows in sources:
        for half in range(2):
            got = lane_gather(rows[:, 128 * half : 128 * half + 128], lanes)
            result = jnp.where(place == 2 * tile + half, got, result)
    return result


def iota(shape, axis):
    return lax.broadcasted_iota(jnp.int32, shape, axis)


def build_kernel(info, *refs):
    sources, (first, second, fold_rows, slots), held, done = refs[:7], refs[7:11], refs[11:18], refs[18]
    copies = [pltpu.make_async_copy(a, b, done.at[i]) for i, (a, b) in enumerate(zip(sources, held))]
    for copy in copies:
        copy.start()
    for copy in copies:
        copy.wait()
    tracers, east, north, levels, weights, indices, flux = held
    for tracer in range(2):
        for quarter in range(4):
            cut = flux[tracer : tracer + 1, 128 * quarter : 128 * quarter + 128]
            slots[:, 4 * tracer + quarter, :] = jnp.broadcast_to(cut, (128, 128))

    def write(out, rows, near, fifth):
        for tracer in range(2):
            out[16 * tracer : 16 * tracer + 16] = tracers[tracer, :, rows, :]
        for half in range(2):
            levels_in, rows_out = slice(8 * half, 8 * half + 8), slice(4 * half, 4 * half + 4)
            out[32:40, rows_out, :] = east[levels_in, near, :]
            out[40:48, rows_out, :] = north[levels_in, near, :]
            out[53 + half] = north[levels_in, fifth, :]
        out[48:52, 0:4, :] = weights[:, near, :]
        out[48:52, 4:8, :] = indices[:, near, :].astype(F32)
        out[52] = levels[rows, :].astype(F32)
        out[55:PLANES] = jnp.zeros((PLANES - 55, H, 256), F32)

    southward, northward = (slice(0, 8), slice(0, 4), 4), (slice(8, 16), slice(12, 16), 11)
    is_odd = info[6] == 1

    @pl.when(is_odd)
    def _():
        write(first, *southward)
        write(second, *northward)

    @pl.when(jnp.logical_not(is_odd))
    def _():
        write(first, *northward)
        write(second, *southward)

    for r in range(2):
        for tracer in range(2):
            at = 4 * r + 2 * tracer
            for part in range(2):
                fold_rows[at + part] = tracers[tracer, 8 * part : 8 * part + 8, 15 - r, :]
        wet = levels[15 - r : 16 - r, :] > 0
        for j in range(4):
            weight = weights[j, 15 - r : 16 - r, :]
            fold_rows[8 + r, j : j + 1, :] = jnp.where(wet, weight, jnp.zeros_like(weight))
            fold_rows[8 + r, 4 + j : 5 + j, :] = indices[j, 15 - r : 16 - r, :].astype(F32)

    @pl.when(info[1] == 1)
    def _():
        second[0:10] = fold_rows[...]


class Sides:
    def __init__(self, info, first, second):
        self.odd, self.top = info[6] == 1, info[1] == 1
        self.first, self.second = first, second

    def blocks(self, plane, cut):
        first, second = self.first[plane, :, cut], self.second[plane, :, cut]
        north = jnp.where(self.top, 0.0, jnp.where(self.odd, second, first))
        return jnp.where(self.odd, first, second), north

    def whole(self, plane, centre, cut=slice(None)):
        south, north = self.blocks(plane, cut)
        return jnp.concatenate([south, centre, north], axis=0)

    def near(self, plane, upper, centre, cut=slice(None)):
        south, north = self.blocks(plane, cut)
        turned_south, turned_north = pltpu.roll(south, 4, 0), pltpu.roll(north, 4, 0)
        if isinstance(upper, bool):
            south, north = (south, turned_north) if upper else (turned_south, north)
        else:
            south, north = jnp.where(upper, south, turned_south), jnp.where(upper, turned_north, north)
        return jnp.concatenate([south, centre, north], axis=0)

    def velocity(self, first_plane, k, centre, cut=slice(None)):
        if isinstance(k, int):
            return self.near(first_plane + k % 8, k >= 8, centre, cut)
        return self.near(first_plane + jnp.bitwise_and(k, 7), k >= 8, centre, cut)

    def north_velocity(self, k, centre, cut=slice(None)):
        got = self.velocity(40, k, centre, cut)
        plane, at = (53 + k // 8, k % 8) if isinstance(k, int) else (53 + jnp.right_shift(k, 3), jnp.bitwise_and(k, 7))
        row = pl.ds(at, 1)
        fifth = jnp.where(self.odd, self.first[plane, row, cut], self.second[plane, row, cut])
        return jnp.where(iota(got.shape, 0) == 3, fifth, got)


def pack_kernel(info, tracers, east, north, levels, weights, indices, partner, first, second, fold_b, ghosts, to_west, to_east):
    is_top = info[1] == 1
    wanted = jnp.broadcast_to(partner[...], (8, 256))
    for block in range(10):
        rows = pl.ds(8 * block, 8)
        sources = [(info[2], second[block]), (info[3], fold_b[block])]
        for half in range(2):
            cut = slice(128 * half, 128 * half + 128)
            ghosts[rows, cut] = pick_columns(wanted[:, cut], sources)
    lane = iota((32, 128), 1)
    row = iota((32, 128), 0)
    ghost_first = jnp.logical_and(row == 24, is_top)
    ghost_second = jnp.logical_and(row == 25, is_top)
    last_north = jnp.logical_and(row == 23, is_top)
    beyond = jnp.logical_and(row >= 24, is_top)
    west_cut, east_cut = slice(0, 128), slice(128, 256)

    sides = Sides(info, first, second)
    whole = sides.whole

    def value(plane, cut):
        if plane < 32:
            got = whole(plane, tracers[plane // 16, plane % 16, :, cut], cut)
            got = jnp.where(ghost_first, ghosts[plane : plane + 1, cut], got)
            return jnp.where(ghost_second, ghosts[32 + plane : 33 + plane, cut], got)
        if plane < 48:
            return sides.velocity(32, plane - 32, east[plane - 32, :, cut], cut)
        if plane < 64:
            return jnp.where(last_north, 0.0, sides.north_velocity(plane - 48, north[plane - 48, :, cut], cut))
        if plane < 72:
            centre = weights[plane - 64, :, cut] if plane < 68 else indices[plane - 68, :, cut].astype(F32)
            got = sides.near(48 + plane % 4, plane >= 68, centre, cut)
            got = jnp.where(ghost_first, ghosts[plane : plane + 1, cut], got)
            return jnp.where(ghost_second, ghosts[plane + 8 : plane + 9, cut], got)
        if plane == 72:
            return jnp.where(beyond, 16.0, whole(52, levels[:, cut].astype(F32), cut))
        return jnp.broadcast_to(partner[:, cut].astype(F32), (32, 128))

    for group in range(5):
        westward = jnp.zeros((32, 128), F32)
        eastward = jnp.zeros((32, 128), F32)
        for slot in range(16 if group < 4 else 10):
            mine = jnp.logical_and(lane >= 8 * slot, lane < 8 * slot + 8)
            plane = 16 * group + slot
            near = value(plane, west_cut)
            far = value(plane, east_cut)
            westward = jnp.where(mine, pltpu.roll(near, 8 * slot, 1) if slot else near, westward)
            eastward = jnp.where(mine, pltpu.roll(far, (8 * slot + 8) % 128, 1) if slot != 15 else far, eastward)
        to_west[group] = westward
        to_east[group] = eastward


def one_hot_lookup(split_table, high, low, count):
    short = lambda v: jnp.broadcast_to(v, (512, count)).astype(jnp.int16)
    matches = lax.broadcasted_iota(jnp.int16, (512, count), 0) == short(high)
    chosen = jnp.where(matches, jnp.bfloat16(1), jnp.bfloat16(0))
    got = jnp.dot(split_table[...], chosen, preferred_element_type=F32)
    lanes = iota((128, count), 0) == low
    first = jnp.sum(jnp.where(lanes, got[:128] + got[128:256], 0.0), axis=0, keepdims=True)
    second = jnp.sum(jnp.where(lanes, got[256:384] + got[384:], 0.0), axis=0, keepdims=True)
    return first, second


def split_place(index):
    high = jnp.bitwise_and(jnp.right_shift(index, 7), 3) * 128 + jnp.right_shift(index, 9)
    return high, jnp.bitwise_and(index, 127)


def split_kernel_table(table, split_table):
    for tracer in range(2):
        for quarter in range(4):
            block = table[:, tracer * 4 + quarter, :].T
            top = block.astype(jnp.bfloat16)
            rest = (block - top.astype(F32)).astype(jnp.bfloat16)
            cut = slice(128 * quarter, 128 * quarter + 128)
            split_table[tracer * 256 : tracer * 256 + 128, cut] = top
            split_table[tracer * 256 + 128 : tracer * 256 + 256, cut] = rest


def halo_tile(from_east, from_west, lane, group, slot):
    shift = (lambda v: v % 128) if isinstance(slot, int) else (lambda v: lax.rem(v, 128))
    near = pltpu.roll(from_east[group], shift(128 - 8 * slot), 1)
    far = pltpu.roll(from_west[group], shift(248 - 8 * slot), 1)
    return jnp.where(lane < 8, near, jnp.where(lane >= 120, far, 0.0))


def lookup_kernel(groups, splits, last, info, table, *rest):
    if splits:
        weights, indices, first, second, ghosts, surface, split_table, high, low, weight = rest
        split_kernel_table(table, split_table)
        is_top = info[1] == 1
        near = Sides(info, first, second).near
        row = iota((32, 256), 0)
        for j in range(4):
            index = near(48 + j, True, indices[j].astype(F32))
            scale = near(48 + j, False, weights[j])
            for r in range(2):
                ghost = jnp.logical_and(row == 24 + r, is_top)
                scale = jnp.where(ghost, ghosts[64 + 8 * r + j : 65 + 8 * r + j, :], scale)
                index = jnp.where(ghost, ghosts[68 + 8 * r + j : 69 + 8 * r + j, :], index)
            high[j], low[j] = split_place(index.astype(jnp.int32))
            weight[j] = scale
    else:
        split_table = table
        if last:
            high, low, weight, from_east, from_west, surface, halo_surface = rest
        else:
            high, low, weight, surface = rest
    def look_up(i, group, count):
        totals = [[jnp.zeros((1, 256), F32) for _ in range(count)] for _ in range(2)]
        rows = [slice(4 * group + q, 4 * group + q + 1) for q in range(count)]
        for j in range(4):
            join = lambda ref: jnp.concatenate([ref[j, r, :] for r in rows], axis=1)
            pair = one_hot_lookup(split_table, join(high), join(low), 256 * count)
            for q, r in enumerate(rows):
                for tracer in range(2):
                    totals[tracer][q] += weight[j, r, :] * pair[tracer][:, 256 * q : 256 * q + 256]
        for tracer in range(2):
            for q in range(count):
                surface[tracer, 4 * i + q : 4 * i + q + 1, :] = totals[tracer][q]

    if last:
        surface[...] = jnp.zeros(surface.shape, F32)
        pl.when(info[1] == 1)(lambda: look_up(0, groups[0], 2))
        pl.when(info[1] != 1)(lambda: look_up(0, groups[0], 4))
    else:
        for i, group in enumerate(groups):
            look_up(i, group, 4)
    if last:
        lane = iota((32, 128), 1)
        small_lane, small_row = iota((16, 128), 1), iota((16, 128), 0)
        places, scales = [], []
        for j in range(4):
            index = halo_tile(from_east, from_west, lane, 4, 4 + j)
            scale = halo_tile(from_east, from_west, lane, 4, j)
            for part in range(2):
                cut = slice(16 * part, 16 * part + 16)
                places.append(spread_rows(index[cut], small_row, small_lane).astype(jnp.int32))
                scales.append(spread_rows(scale[cut], small_row, small_lane))
        halo_high, halo_low = split_place(jnp.concatenate(places, axis=1))
        pair = one_hot_lookup(split_table, halo_high, halo_low, 1024)
        for tracer in range(2):
            for part in range(2):
                total = jnp.zeros((1, 128), F32)
                for j in range(4):
                    at = 2 * j + part
                    total += scales[at] * pair[tracer][:, 128 * at : 128 * at + 128]
                halo_surface[tracer, 16 * part : 16 * part + 16, :] = gather_rows(total, small_row, small_lane)


def spread_rows(halo, row_of, lane):
    moved = jnp.where(lane < 8, pltpu.roll(halo, 4, 1), jnp.zeros_like(halo))
    for shift in (8, 16, 32, 64):
        moved = moved + pltpu.roll(moved, shift, 1)
    return jnp.sum(jnp.where(lane // 8 == row_of, moved, jnp.zeros_like(moved)), axis=0, keepdims=True)


def gather_rows(packed, row_of, lane):
    moved = jnp.where(lane // 8 == row_of, jnp.broadcast_to(packed, (16, 128)), 0.0)
    for shift in (8, 16, 32, 64):
        moved = moved + pltpu.roll(moved, shift, 1)
    return pltpu.roll(moved, 124, 1)


def east_of(f):
    return pltpu.roll(f, f.shape[1] - 1, 1)


def west_of(f):
    return pltpu.roll(f, 1, 1)


def north_of(f):
    return pltpu.roll(f, f.shape[0] - 1, 0)


def south_of(f):
    return pltpu.roll(f, 1, 0)


def run_levels(cells, half_east, half_north, depth, surface, store, window=slice(0, 32), keep=slice(0, 32), tracers=(0, 1), unroll=2):
    depth = depth[window, :]
    east_depth = jnp.minimum(depth, east_of(depth))
    north_depth = jnp.minimum(depth, north_of(depth))
    kept = slice(window.start + keep.start, window.start + keep.stop)

    def body(k, carry):
        level = k.astype(F32)
        east_open, north_open, wet = level < east_depth, level < north_depth, level < depth[keep]
        deeper = level + 1.0 < depth[keep]
        east, north = half_east[k, window, :], half_north[k, window, :]
        above, under = jnp.minimum(k + 1, 15), jnp.maximum(k - 1, 0)
        at_surface = jnp.where(k == 0, 0.5, 0.0).astype(F32)
        for tracer in tracers:
            here = cells[tracer, k]
            to_east, to_north = east_of(here), north_of(here)
            grad_east = jnp.where(east_open, to_east - here, 0.0)
            grad_north = jnp.where(north_open, to_north - here, 0.0)
            lap = grad_east - west_of(grad_east) + (grad_north - south_of(grad_north))
            flat = 0.08 * here - 0.01 * lap
            flux_east = jnp.where(east_open, east_of(flat) - flat - east * (to_east + here), 0.0)
            flux_north = jnp.where(north_open, north_of(flat) - flat - north * (to_north + here), 0.0)
            total = (flux_east - west_of(flux_east) + (flux_north - south_of(flux_north)))[keep]
            centre = here[keep]
            vertical = jnp.where(deeper, cells[tracer, above, keep, :] - centre, 0.0)
            total += 0.1 * (vertical - (centre - cells[tracer, under, keep, :]))
            if surface is not None:
                total += at_surface * surface[tracer, kept, :]
            store(tracer, k, centre + jnp.where(wet, total, 0.0))
        return carry

    lax.fori_loop(0, 16, body, 0, unroll=unroll)


def keep_step(cells_out, fold_out):
    def store(tracer, k, fresh):
        cells_out[tracer, k] = fresh
        for r in range(2):
            fold_out[pl.ds(32 * r + 16 * tracer + k, 1), :] = fresh[23 - r : 24 - r, 0:256]

    return store


def place_ghosts(cells, ghosts, columns, row=24):
    def place(k, carry):
        for tracer in range(2):
            for r in range(2):
                cells[tracer, k, row + r : row + r + 1, 0:columns] = ghosts[pl.ds(32 * r + 16 * tracer + k, 1), :]
        return carry

    lax.fori_loop(0, 16, place, 0)


def first_kernel(
    info, tracers, east, north, levels, partner, first, second, ghosts, from_east, from_west,
    cells_out, fold_out, east_ext, north_ext, depth_ext, partner_ext, start,
):
    is_top = info[1] == 1
    lane = iota((32, 128), 1)
    row = iota((32, 256), 0)
    last_north = jnp.logical_and(row == 23, is_top)
    halo = functools.partial(halo_tile, from_east, from_west, lane)

    sides = Sides(info, first, second)
    whole = sides.whole

    def fill(k, carry):
        for tracer in range(2):
            start[tracer, k, :, 0:256] = whole(tracer * 16 + k, tracers[tracer, k])
            start[tracer, k, :, 256:384] = halo(tracer, k)
        east_ext[k, :, 0:256] = 0.5 * sides.velocity(32, k, east[k])
        east_ext[k, :, 256:384] = 0.5 * halo(2, k)
        north_ext[k, :, 0:256] = jnp.where(last_north, 0.0, 0.5 * sides.north_velocity(k, north[k]))
        north_ext[k, :, 256:384] = 0.5 * halo(3, k)
        return carry

    lax.fori_loop(0, 16, fill, 0)

    @pl.when(is_top)
    def _():
        place_ghosts(start, ghosts, 256)

    depth_ext[:, 0:256] = jnp.where(
        jnp.logical_and(row >= 24, is_top), 16.0, whole(52, levels[...].astype(F32))
    )
    depth_ext[:, 256:384] = halo(4, 8)
    partner_ext[:, 0:256] = jnp.broadcast_to(partner[...], (8, 256))
    partner_ext[:, 256:384] = halo(4, 9)[0:8].astype(jnp.int32)
    run_levels(start, east_ext, north_ext, depth_ext, None, keep_step(cells_out, fold_out))


def fold_ghosts(info, partner_ext, received, ghosts):
    def block_body(block, carry):
        rows = pl.ds(pl.multiple_of(8 * block, 8), 8)
        all_sources = [(info[2 + i], ref[rows, :]) for i, ref in enumerate(received)]
        for part, sources in enumerate((all_sources[:2], all_sources[:2], all_sources)):
            cut = slice(128 * part, 128 * part + 128)
            ghosts[rows, cut] = pick_columns(partner_ext[:, cut], sources)
        return carry

    lax.fori_loop(0, 8, block_body, 0)


def second_kernel(
    info, cells, east_ext, north_ext, depth_ext, partner_ext, fold_a, fold_b, fold_c, fold_d, surface_a, surface_b, surface_c, surface_d,
    surface_e, halo_surface, cells_out, fold_out, surface_ext, ghosts, start,
):
    def fill(k, carry):
        for tracer in range(2):
            start[tracer, k] = cells[tracer, k]
        return carry

    lax.fori_loop(0, 16, fill, 0)

    @pl.when(info[1] == 1)
    def _():
        fold_ghosts(info, partner_ext, (fold_a, fold_b, fold_c, fold_d), ghosts)
        place_ghosts(start, ghosts, 384)

    surface_ext[...] = jnp.zeros((2, 32, 384), F32)
    for tracer in range(2):
        at = 4
        for piece in (surface_a, surface_b, surface_c, surface_d, surface_e):
            surface_ext[tracer, at : at + piece.shape[1], 0:256] = piece[tracer]
            at += piece.shape[1]
        surface_ext[tracer, :, 256:384] = halo_surface[tracer]
        start[tracer, 0] = start[tracer, 0] + jnp.where(depth_ext[...] > 0.0, 0.5 * surface_ext[tracer], 0.0)
    run_levels(start, east_ext, north_ext, depth_ext, surface_ext, keep_step(cells_out, fold_out))


def last_kernel(
    info, cells, east_ext, north_ext, depth_ext, partner_ext, fold_a, fold_b, fold_c, fold_d, surface_ext, result, ghosts, start
):
    def fill(k, carry):
        for tracer in range(2):
            start[tracer, k] = cells[tracer, k]
        return carry

    lax.fori_loop(0, 16, fill, 0)

    @pl.when(info[1] == 1)
    def _():
        fold_ghosts(info, partner_ext, (fold_a, fold_b, fold_c, fold_d), ghosts)
        place_ghosts(start, ghosts, 384)

    def store(tracer, k, fresh):
        result[tracer, k] = fresh[:, 0:256]

    run_levels(start, east_ext, north_ext, depth_ext, surface_ext, store, keep=slice(8, 24), unroll=4)


def call(kernel, ins, outs, scratch=(), cost=None, earlier=(), ins_any=False, outs_any=False, alias=None, params=PARAMS):
    used = len(ins)

    def body(*refs):
        kernel(own_place(), *refs[:used], *refs[used + len(earlier) :])

    anywhere = pl.BlockSpec(memory_space=pl.ANY)
    hbm = pl.BlockSpec(memory_space=pltpu.HBM)

    def place(i, v):
        return hbm if ins_any or i == alias else anywhere if i >= used else VMEM

    arrays = tuple(ins) + tuple(earlier)
    return pl.pallas_call(
        body,
        out_shape=tuple(jax.ShapeDtypeStruct(s, d) for s, d in outs),
        in_specs=[place(i, v) for i, v in enumerate(arrays)],
        out_specs=tuple(hbm if outs_any else VMEM for _ in outs),
        scratch_shapes=list(scratch),
        compiler_params=params,
        cost_estimate=cost,
        input_output_aliases={} if alias is None else {alias: 0},
    )(*arrays)


STEP_COST = pl.CostEstimate(flops=10**7, bytes_accessed=16 * 2**20, transcendentals=0)


def lookup_cost(groups):
    return pl.CostEstimate(flops=groups * 2 * 512 * 512 * 4096, bytes_accessed=groups * 2**20, transcendentals=0)


def per_device(tracers, east, north, levels, partner, atm_flux, indices, weights):
    nlon, nlat = lax.axis_size("lon"), lax.axis_size("lat")
    both = ("lon", "lat")
    top = nlat - 1

    def fold_permute(rows, d):
        pairs = [(i * nlat + top, ((nlon - 1 + d - i) % nlon) * nlat + top) for i in range(nlon)]
        return lax.ppermute(rows, both, pairs)

    message = ((PLANES, H, 256), F32)
    whole_inputs = (tracers, east, north, levels, weights, indices)
    build_inputs = (*whole_inputs, atm_flux)
    first, second, fold_rows, slots = call(
        build_kernel,
        build_inputs,
        [message, message, ((10, 8, 256), F32), ((nlon * nlat, 8, 128), F32)],
        [pltpu.VMEM(a.shape, a.dtype) for a in build_inputs] + [pltpu.SemaphoreType.DMA((7,))],
        ins_any=True,
        params=pltpu.CompilerParams(vmem_limit_bytes=60 * 2**20),
    )
    def after(value, *earlier):
        return lax.optimization_barrier((value, *earlier))[0]

    swaps = [(i, i + 1) for i in range(0, nlat, 2)]
    first = lax.ppermute(first, "lat", swaps + [(j, i) for i, j in swaps])
    swaps = [(i, i + 1) for i in range(1, nlat - 1, 2)]
    swaps = [(c * nlat + i, c * nlat + j) for c in range(nlon) for i, j in swaps + [(j, i) for i, j in swaps]]
    facing = [(c * nlat + top, (nlon - 1 - c) * nlat + top) for c in range(nlon)]
    second = lax.ppermute(second, both, swaps + facing)
    fold_b = fold_permute(fold_rows, 1)

    table = lax.all_to_all(slots, both, 0, 0, tiled=True)

    partner_row = partner.reshape(1, -1)
    ghosts, to_west, to_east = call(
        pack_kernel,
        (*whole_inputs, partner_row, first, second, fold_b),
        [((80, 256), F32), ((5, 32, 128), F32), ((5, 32, 128), F32)],
    )
    from_east = lax.ppermute(to_west, "lon", [((i + 1) % nlon, i) for i in range(nlon)])
    from_west = lax.ppermute(to_east, "lon", [(i, (i + 1) % nlon) for i in range(nlon)])

    def lookups(groups, ins, splits=False, last=False, earlier=()):
        outs = [((2, 4 * len(groups), 256), F32)]
        places = ((4, 32, 256), jnp.int32)
        outs += [((512, 512), jnp.bfloat16), places, places, (places[0], F32)] if splits else []
        outs += [((2, 32, 128), F32)] if last else []
        return call(
            functools.partial(lookup_kernel, groups, splits, last), ins, outs, (), lookup_cost(len(groups)), earlier
        )

    surface_a, *places = lookups((1, 2), (table, weights, indices, first, second, ghosts), splits=True)

    wide = (2, 16, 32, 384)
    cells, fold_rows, east_ext, north_ext, depth_ext, partner_ext = call(
        first_kernel,
        (tracers, east, north, levels, partner_row, first, second, ghosts, from_east, from_west),
        [(wide, F32), ((64, 256), F32), (wide[1:], F32), (wide[1:], F32), ((32, 384), F32), ((8, 384), jnp.int32)],
        [pltpu.VMEM(wide, F32)],
        STEP_COST,
        (surface_a,),
    )
    statics = (east_ext, north_ext, depth_ext)
    received = [fold_permute(fold_rows, 0)]
    (surface_b,) = lookups((3,), places, earlier=(fold_rows,))
    received.append(fold_permute(after(fold_rows, surface_b), 1))
    (surface_c,) = lookups((4,), places, earlier=(received[0], surface_b))
    received.append(fold_permute(after(fold_rows, surface_c), -1))
    (surface_d,) = lookups((5,), places, earlier=(received[1], surface_c))
    received.append(fold_permute(after(fold_rows, surface_d), 2))
    surface_e, halo_surface = lookups((6,), (*places, from_east, from_west), last=True, earlier=(received[2], surface_d))

    ghost_rows = pltpu.VMEM((64, 384), F32)
    cells, fold_rows, surface_ext = call(
        second_kernel,
        (cells, *statics, partner_ext, *received, surface_a, surface_b, surface_c, surface_d, surface_e,
         halo_surface),
        [(wide, F32), ((64, 256), F32), ((2, 32, 384), F32)],
        [ghost_rows, pltpu.VMEM(wide, F32)],
        STEP_COST,
    )
    received = [fold_permute(fold_rows, d) for d in (0, 1, -1, 2)]
    (result,) = call(
        last_kernel,
        (cells, *statics, partner_ext, *received, surface_ext),
        [(tracers.shape, F32)],
        [ghost_rows, pltpu.VMEM(wide, F32)],
        STEP_COST,
    )
    return result


def solution(mesh):
    return jax.shard_map(
        per_device,
        mesh=mesh,
        in_specs=(
            P(None, None, "lat", "lon"),
            P(None, "lat", "lon"),
            P(None, "lat", "lon"),
            P("lat", "lon"),
            P("lon"),
            P(None, ("lon", "lat")),
            P(None, "lat", "lon"),
            P(None, "lat", "lon"),
        ),
        out_specs=P(None, None, "lat", "lon"),
        check_vma=False,
    )
```

```python
import functools

import jax
import jax.numpy as jnp
from jax import lax
from jax.experimental import pallas as pl
from jax.experimental.pallas import tpu as pltpu
from jax.sharding import PartitionSpec as P

H = 8
PLANES = 64
VMEM = pl.BlockSpec(memory_space=pltpu.VMEM)
PARAMS = pltpu.CompilerParams(vmem_limit_bytes=20 * 2**20)
F32 = jnp.float32
LANE_GATHER = lax.GatherDimensionNumbers(
    offset_dims=(),
    collapsed_slice_dims=(1,),
    start_index_map=(1,),
    operand_batching_dims=(0,),
    start_indices_batching_dims=(0,),
)


def lane_gather(values, lanes):
    return lax.gather(
        values, lanes[..., None], LANE_GATHER, (1, 1), mode=lax.GatherScatterMode.PROMISE_IN_BOUNDS
    )


def own_place():
    nlon, nlat = lax.axis_size("lon"), lax.axis_size("lat")
    t, lat = lax.axis_index("lon"), lax.axis_index("lat")
    tiles = [lax.rem(2 * nlon - 1 - t + d, nlon) for d in (0, 1, -1, 2)]
    return [t, (lat == nlat - 1).astype(jnp.int32), *tiles, lax.rem(lat, 2)]


def pick_columns(partner, sources):
    lanes = jnp.bitwise_and(partner, 127)
    place = jnp.right_shift(partner, 7)
    result = jnp.zeros((8, 128), F32)
    for tile, rows in sources:
        for half in range(2):
            got = lane_gather(rows[:, 128 * half : 128 * half + 128], lanes)
            result = jnp.where(place == 2 * tile + half, got, result)
    return result


def iota(shape, axis):
    return lax.broadcasted_iota(jnp.int32, shape, axis)


def build_kernel(info, *refs):
    sources, (first, second, fold_rows, slots), held, done = refs[:7], refs[7:11], refs[11:18], refs[18]
    copies = [pltpu.make_async_copy(a, b, done.at[i]) for i, (a, b) in enumerate(zip(sources, held))]
    for copy in copies:
        copy.start()
    for copy in copies:
        copy.wait()
    tracers, east, north, levels, weights, indices, flux = held
    for tracer in range(2):
        for quarter in range(4):
            cut = flux[tracer : tracer + 1, 128 * quarter : 128 * quarter + 128]
            slots[:, 4 * tracer + quarter, :] = jnp.broadcast_to(cut, (128, 128))

    def write(out, rows, near, fifth):
        for tracer in range(2):
            out[16 * tracer : 16 * tracer + 16] = tracers[tracer, :, rows, :]
        for half in range(2):
            levels_in, rows_out = slice(8 * half, 8 * half + 8), slice(4 * half, 4 * half + 4)
            out[32:40, rows_out, :] = east[levels_in, near, :]
            out[40:48, rows_out, :] = north[levels_in, near, :]
            out[53 + half] = north[levels_in, fifth, :]
        out[48:52, 0:4, :] = weights[:, near, :]
        out[48:52, 4:8, :] = indices[:, near, :].astype(F32)
        out[52] = levels[rows, :].astype(F32)
        out[55:PLANES] = jnp.zeros((PLANES - 55, H, 256), F32)

    southward, northward = (slice(0, 8), slice(0, 4), 4), (slice(8, 16), slice(12, 16), 11)
    is_odd = info[6] == 1

    @pl.when(is_odd)
    def _():
        write(first, *southward)
        write(second, *northward)

    @pl.when(jnp.logical_not(is_odd))
    def _():
        write(first, *northward)
        write(second, *southward)

    for r in range(2):
        for tracer in range(2):
            at = 4 * r + 2 * tracer
            for part in range(2):
                fold_rows[at + part] = tracers[tracer, 8 * part : 8 * part + 8, 15 - r, :]
        wet = levels[15 - r : 16 - r, :] > 0
        for j in range(4):
            weight = weights[j, 15 - r : 16 - r, :]
            fold_rows[8 + r, j : j + 1, :] = jnp.where(wet, weight, jnp.zeros_like(weight))
            fold_rows[8 + r, 4 + j : 5 + j, :] = indices[j, 15 - r : 16 - r, :].astype(F32)

    @pl.when(info[1] == 1)
    def _():
        second[0:10] = fold_rows[...]


class Sides:
    def __init__(self, info, first, second):
        self.odd, self.top = info[6] == 1, info[1] == 1
        self.first, self.second = first, second

    def blocks(self, plane, cut):
        first, second = self.first[plane, :, cut], self.second[plane, :, cut]
        north = jnp.where(self.top, 0.0, jnp.where(self.odd, second, first))
        return jnp.where(self.odd, first, second), north

    def whole(self, plane, centre, cut=slice(None)):
        south, north = self.blocks(plane, cut)
        return jnp.concatenate([south, centre, north], axis=0)

    def near(self, plane, upper, centre, cut=slice(None)):
        south, north = self.blocks(plane, cut)
        turned_south, turned_north = pltpu.roll(south, 4, 0), pltpu.roll(north, 4, 0)
        if isinstance(upper, bool):
            south, north = (south, turned_north) if upper else (turned_south, north)
        else:
            south, north = jnp.where(upper, south, turned_south), jnp.where(upper, turned_north, north)
        return jnp.concatenate([south, centre, north], axis=0)

    def velocity(self, first_plane, k, centre, cut=slice(None)):
        if isinstance(k, int):
            return self.near(first_plane + k % 8, k >= 8, centre, cut)
        return self.near(first_plane + jnp.bitwise_and(k, 7), k >= 8, centre, cut)

    def north_velocity(self, k, centre, cut=slice(None)):
        got = self.velocity(40, k, centre, cut)
        plane, at = (53 + k // 8, k % 8) if isinstance(k, int) else (53 + jnp.right_shift(k, 3), jnp.bitwise_and(k, 7))
        row = pl.ds(at, 1)
        fifth = jnp.where(self.odd, self.first[plane, row, cut], self.second[plane, row, cut])
        return jnp.where(iota(got.shape, 0) == 3, fifth, got)


def pack_kernel(info, tracers, east, north, levels, weights, indices, partner, first, second, fold_b, ghosts, to_west, to_east):
    is_top = info[1] == 1
    wanted = jnp.broadcast_to(partner[...], (8, 256))
    for block in range(10):
        rows = pl.ds(8 * block, 8)
        sources = [(info[2], second[block]), (info[3], fold_b[block])]
        for half in range(2):
            cut = slice(128 * half, 128 * half + 128)
            ghosts[rows, cut] = pick_columns(wanted[:, cut], sources)
    lane = iota((32, 128), 1)
    row = iota((32, 128), 0)
    ghost_first = jnp.logical_and(row == 24, is_top)
    ghost_second = jnp.logical_and(row == 25, is_top)
    last_north = jnp.logical_and(row == 23, is_top)
    beyond = jnp.logical_and(row >= 24, is_top)
    west_cut, east_cut = slice(0, 128), slice(128, 256)

    sides = Sides(info, first, second)
    whole = sides.whole

    def value(plane, cut):
        if plane < 32:
            got = whole(plane, tracers[plane // 16, plane % 16, :, cut], cut)
            got = jnp.where(ghost_first, ghosts[plane : plane + 1, cut], got)
            return jnp.where(ghost_second, ghosts[32 + plane : 33 + plane, cut], got)
        if plane < 48:
            return sides.velocity(32, plane - 32, east[plane - 32, :, cut], cut)
        if plane < 64:
            return jnp.where(last_north, 0.0, sides.north_velocity(plane - 48, north[plane - 48, :, cut], cut))
        if plane < 72:
            centre = weights[plane - 64, :, cut] if plane < 68 else indices[plane - 68, :, cut].astype(F32)
            got = sides.near(48 + plane % 4, plane >= 68, centre, cut)
            got = jnp.where(ghost_first, ghosts[plane : plane + 1, cut], got)
            return jnp.where(ghost_second, ghosts[plane + 8 : plane + 9, cut], got)
        if plane == 72:
            return jnp.where(beyond, 16.0, whole(52, levels[:, cut].astype(F32), cut))
        return jnp.broadcast_to(partner[:, cut].astype(F32), (32, 128))

    for group in range(5):
        westward = jnp.zeros((32, 128), F32)
        eastward = jnp.zeros((32, 128), F32)
        for slot in range(16 if group < 4 else 10):
            mine = jnp.logical_and(lane >= 8 * slot, lane < 8 * slot + 8)
            plane = 16 * group + slot
            near = value(plane, west_cut)
            far = value(plane, east_cut)
            westward = jnp.where(mine, pltpu.roll(near, 8 * slot, 1) if slot else near, westward)
            eastward = jnp.where(mine, pltpu.roll(far, (8 * slot + 8) % 128, 1) if slot != 15 else far, eastward)
        to_west[group] = westward
        to_east[group] = eastward


def one_hot_lookup(split_table, high, low, count):
    short = lambda v: jnp.broadcast_to(v, (512, count)).astype(jnp.int16)
    matches = lax.broadcasted_iota(jnp.int16, (512, count), 0) == short(high)
    chosen = jnp.where(matches, jnp.bfloat16(1), jnp.bfloat16(0))
    got = jnp.dot(split_table[...], chosen, preferred_element_type=F32)
    lanes = iota((128, count), 0) == low
    first = jnp.sum(jnp.where(lanes, got[:128] + got[128:256], 0.0), axis=0, keepdims=True)
    second = jnp.sum(jnp.where(lanes, got[256:384] + got[384:], 0.0), axis=0, keepdims=True)
    return first, second


def split_place(index):
    high = jnp.bitwise_and(jnp.right_shift(index, 7), 3) * 128 + jnp.right_shift(index, 9)
    return high, jnp.bitwise_and(index, 127)


def split_kernel_table(table, split_table):
    for tracer in range(2):
        for quarter in range(4):
            block = table[:, tracer * 4 + quarter, :].T
            top = block.astype(jnp.bfloat16)
            rest = (block - top.astype(F32)).astype(jnp.bfloat16)
            cut = slice(128 * quarter, 128 * quarter + 128)
            split_table[tracer * 256 : tracer * 256 + 128, cut] = top
            split_table[tracer * 256 + 128 : tracer * 256 + 256, cut] = rest


def halo_tile(from_east, from_west, lane, group, slot):
    shift = (lambda v: v % 128) if isinstance(slot, int) else (lambda v: lax.rem(v, 128))
    near = pltpu.roll(from_east[group], shift(128 - 8 * slot), 1)
    far = pltpu.roll(from_west[group], shift(248 - 8 * slot), 1)
    return jnp.where(lane < 8, near, jnp.where(lane >= 120, far, 0.0))


def lookup_kernel(groups, splits, last, info, table, *rest):
    if splits:
        weights, indices, first, second, ghosts, surface, split_table, high, low, weight = rest
        split_kernel_table(table, split_table)
        is_top = info[1] == 1
        near = Sides(info, first, second).near
        row = iota((32, 256), 0)
        for j in range(4):
            index = near(48 + j, True, indices[j].astype(F32))
            scale = near(48 + j, False, weights[j])
            for r in range(2):
                ghost = jnp.logical_and(row == 24 + r, is_top)
                scale = jnp.where(ghost, ghosts[64 + 8 * r + j : 65 + 8 * r + j, :], scale)
                index = jnp.where(ghost, ghosts[68 + 8 * r + j : 69 + 8 * r + j, :], index)
            high[j], low[j] = split_place(index.astype(jnp.int32))
            weight[j] = scale
    else:
        split_table = table
        if last:
            high, low, weight, from_east, from_west, surface, halo_surface = rest
        else:
            high, low, weight, surface = rest
    def look_up(i, group, count):
        totals = [[jnp.zeros((1, 256), F32) for _ in range(count)] for _ in range(2)]
        rows = [slice(4 * group + q, 4 * group + q + 1) for q in range(count)]
        for j in range(4):
            join = lambda ref: jnp.concatenate([ref[j, r, :] for r in rows], axis=1)
            pair = one_hot_lookup(split_table, join(high), join(low), 256 * count)
            for q, r in enumerate(rows):
                for tracer in range(2):
                    totals[tracer][q] += weight[j, r, :] * pair[tracer][:, 256 * q : 256 * q + 256]
        for tracer in range(2):
            for q in range(count):
                surface[tracer, 4 * i + q : 4 * i + q + 1, :] = totals[tracer][q]

    if last:
        surface[...] = jnp.zeros(surface.shape, F32)
        pl.when(info[1] == 1)(lambda: look_up(0, groups[0], 2))
        pl.when(info[1] != 1)(lambda: look_up(0, groups[0], 4))
    else:
        for i, group in enumerate(groups):
            look_up(i, group, 4)
    if last:
        lane = iota((32, 128), 1)
        small_lane, small_row = iota((16, 128), 1), iota((16, 128), 0)
        places, scales = [], []
        for j in range(4):
            index = halo_tile(from_east, from_west, lane, 4, 4 + j)
            scale = halo_tile(from_east, from_west, lane, 4, j)
            for part in range(2):
                cut = slice(16 * part, 16 * part + 16)
                places.append(spread_rows(index[cut], small_row, small_lane).astype(jnp.int32))
                scales.append(spread_rows(scale[cut], small_row, small_lane))
        halo_high, halo_low = split_place(jnp.concatenate(places, axis=1))
        pair = one_hot_lookup(split_table, halo_high, halo_low, 1024)
        for tracer in range(2):
            for part in range(2):
                total = jnp.zeros((1, 128), F32)
                for j in range(4):
                    at = 2 * j + part
                    total += scales[at] * pair[tracer][:, 128 * at : 128 * at + 128]
                halo_surface[tracer, 16 * part : 16 * part + 16, :] = gather_rows(total, small_row, small_lane)


def spread_rows(halo, row_of, lane):
    moved = jnp.where(lane < 8, pltpu.roll(halo, 4, 1), jnp.zeros_like(halo))
    for shift in (8, 16, 32, 64):
        moved = moved + pltpu.roll(moved, shift, 1)
    return jnp.sum(jnp.where(lane // 8 == row_of, moved, jnp.zeros_like(moved)), axis=0, keepdims=True)


def gather_rows(packed, row_of, lane):
    moved = jnp.where(lane // 8 == row_of, jnp.broadcast_to(packed, (16, 128)), 0.0)
    for shift in (8, 16, 32, 64):
        moved = moved + pltpu.roll(moved, shift, 1)
    return pltpu.roll(moved, 124, 1)


def east_of(f):
    return pltpu.roll(f, f.shape[1] - 1, 1)


def west_of(f):
    return pltpu.roll(f, 1, 1)


def north_of(f):
    return pltpu.roll(f, f.shape[0] - 1, 0)


def south_of(f):
    return pltpu.roll(f, 1, 0)


def run_levels(cells, half_east, half_north, depth, surface, store, window=slice(0, 32), keep=slice(0, 32), tracers=(0, 1), unroll=2):
    depth = depth[window, :]
    east_depth = jnp.minimum(depth, east_of(depth))
    north_depth = jnp.minimum(depth, north_of(depth))
    kept = slice(window.start + keep.start, window.start + keep.stop)

    def body(k, carry):
        level = k.astype(F32)
        east_open, north_open, wet = level < east_depth, level < north_depth, level < depth[keep]
        deeper = level + 1.0 < depth[keep]
        east, north = half_east[k, window, :], half_north[k, window, :]
        above, under = jnp.minimum(k + 1, 15), jnp.maximum(k - 1, 0)
        at_surface = jnp.where(k == 0, 0.5, 0.0).astype(F32)
        for tracer in tracers:
            here = cells[tracer, k]
            to_east, to_north = east_of(here), north_of(here)
            grad_east = jnp.where(east_open, to_east - here, 0.0)
            grad_north = jnp.where(north_open, to_north - here, 0.0)
            lap = grad_east - west_of(grad_east) + (grad_north - south_of(grad_north))
            flat = 0.08 * here - 0.01 * lap
            flux_east = jnp.where(east_open, east_of(flat) - flat - east * (to_east + here), 0.0)
            flux_north = jnp.where(north_open, north_of(flat) - flat - north * (to_north + here), 0.0)
            total = (flux_east - west_of(flux_east) + (flux_north - south_of(flux_north)))[keep]
            centre = here[keep]
            vertical = jnp.where(deeper, cells[tracer, above, keep, :] - centre, 0.0)
            total += 0.1 * (vertical - (centre - cells[tracer, under, keep, :]))
            if surface is not None:
                total += at_surface * surface[tracer, kept, :]
            store(tracer, k, centre + jnp.where(wet, total, 0.0))
        return carry

    lax.fori_loop(0, 16, body, 0, unroll=unroll)


def keep_step(cells_out, fold_out):
    def store(tracer, k, fresh):
        cells_out[tracer, k] = fresh
        for r in range(2):
            fold_out[pl.ds(32 * r + 16 * tracer + k, 1), :] = fresh[23 - r : 24 - r, 0:256]

    return store


def place_ghosts(cells, ghosts, columns, row=24):
    def place(k, carry):
        for tracer in range(2):
            for r in range(2):
                cells[tracer, k, row + r : row + r + 1, 0:columns] = ghosts[pl.ds(32 * r + 16 * tracer + k, 1), :]
        return carry

    lax.fori_loop(0, 16, place, 0, unroll=4)


def first_kernel(
    info, tracers, east, north, levels, partner, first, second, ghosts, from_east, from_west,
    cells_out, fold_out, east_ext, north_ext, depth_ext, partner_ext, start,
):
    is_top = info[1] == 1
    lane = iota((32, 128), 1)
    row = iota((32, 256), 0)
    last_north = jnp.logical_and(row == 23, is_top)
    halo = functools.partial(halo_tile, from_east, from_west, lane)

    sides = Sides(info, first, second)
    whole = sides.whole

    def fill(k, carry):
        for tracer in range(2):
            start[tracer, k, :, 0:256] = whole(tracer * 16 + k, tracers[tracer, k])
            start[tracer, k, :, 256:384] = halo(tracer, k)
        east_ext[k, :, 0:256] = 0.5 * sides.velocity(32, k, east[k])
        east_ext[k, :, 256:384] = 0.5 * halo(2, k)
        north_ext[k, :, 0:256] = jnp.where(last_north, 0.0, 0.5 * sides.north_velocity(k, north[k]))
        north_ext[k, :, 256:384] = 0.5 * halo(3, k)
        return carry

    lax.fori_loop(0, 16, fill, 0, unroll=4)

    @pl.when(is_top)
    def _():
        place_ghosts(start, ghosts, 256)

    depth_ext[:, 0:256] = jnp.where(
        jnp.logical_and(row >= 24, is_top), 16.0, whole(52, levels[...].astype(F32))
    )
    depth_ext[:, 256:384] = halo(4, 8)
    partner_ext[:, 0:256] = jnp.broadcast_to(partner[...], (8, 256))
    partner_ext[:, 256:384] = halo(4, 9)[0:8].astype(jnp.int32)
    run_levels(start, east_ext, north_ext, depth_ext, None, keep_step(cells_out, fold_out))


def fold_ghosts(info, partner_ext, received, ghosts):
    def block_body(block, carry):
        rows = pl.ds(pl.multiple_of(8 * block, 8), 8)
        all_sources = [(info[2 + i], ref[rows, :]) for i, ref in enumerate(received)]
        for part, sources in enumerate((all_sources[:2], all_sources[:2], all_sources)):
            cut = slice(128 * part, 128 * part + 128)
            ghosts[rows, cut] = pick_columns(partner_ext[:, cut], sources)
        return carry

    lax.fori_loop(0, 8, block_body, 0, unroll=4)


def second_kernel(
    info, cells, east_ext, north_ext, depth_ext, partner_ext, fold_a, fold_b, fold_c, fold_d, surface_a, surface_b, surface_c, surface_d,
    surface_e, halo_surface, cells_out, fold_out, surface_ext, ghosts, start,
):
    def fill(k, carry):
        for tracer in range(2):
            start[tracer, k] = cells[tracer, k]
        return carry

    lax.fori_loop(0, 16, fill, 0, unroll=4)

    @pl.when(info[1] == 1)
    def _():
        fold_ghosts(info, partner_ext, (fold_a, fold_b, fold_c, fold_d), ghosts)
        place_ghosts(start, ghosts, 384)

    surface_ext[...] = jnp.zeros((2, 32, 384), F32)
    for tracer in range(2):
        at = 4
        for piece in (surface_a, surface_b, surface_c, surface_d, surface_e):
            surface_ext[tracer, at : at + piece.shape[1], 0:256] = piece[tracer]
            at += piece.shape[1]
        surface_ext[tracer, :, 256:384] = halo_surface[tracer]
        start[tracer, 0] = start[tracer, 0] + jnp.where(depth_ext[...] > 0.0, 0.5 * surface_ext[tracer], 0.0)
    run_levels(start, east_ext, north_ext, depth_ext, surface_ext, keep_step(cells_out, fold_out))


def last_kernel(
    info, cells, east_ext, north_ext, depth_ext, partner_ext, fold_a, fold_b, fold_c, fold_d, surface_ext, result, ghosts, start
):
    def fill(k, carry):
        for tracer in range(2):
            start[tracer, k] = cells[tracer, k]
        return carry

    lax.fori_loop(0, 16, fill, 0, unroll=4)

    @pl.when(info[1] == 1)
    def _():
        fold_ghosts(info, partner_ext, (fold_a, fold_b, fold_c, fold_d), ghosts)
        place_ghosts(start, ghosts, 384)

    def store(tracer, k, fresh):
        result[tracer, k] = fresh[:, 0:256]

    run_levels(start, east_ext, north_ext, depth_ext, surface_ext, store, keep=slice(8, 24), unroll=4)


def call(kernel, ins, outs, scratch=(), cost=None, earlier=(), ins_any=False, outs_any=False, alias=None, params=PARAMS):
    used = len(ins)

    def body(*refs):
        kernel(own_place(), *refs[:used], *refs[used + len(earlier) :])

    anywhere = pl.BlockSpec(memory_space=pl.ANY)
    hbm = pl.BlockSpec(memory_space=pltpu.HBM)

    def place(i, v):
        return hbm if ins_any or i == alias else anywhere if i >= used else VMEM

    arrays = tuple(ins) + tuple(earlier)
    return pl.pallas_call(
        body,
        out_shape=tuple(jax.ShapeDtypeStruct(s, d) for s, d in outs),
        in_specs=[place(i, v) for i, v in enumerate(arrays)],
        out_specs=tuple(hbm if outs_any else VMEM for _ in outs),
        scratch_shapes=list(scratch),
        compiler_params=params,
        cost_estimate=cost,
        input_output_aliases={} if alias is None else {alias: 0},
    )(*arrays)


STEP_COST = pl.CostEstimate(flops=10**7, bytes_accessed=16 * 2**20, transcendentals=0)


def lookup_cost(groups):
    return pl.CostEstimate(flops=groups * 2 * 512 * 512 * 4096, bytes_accessed=groups * 2**20, transcendentals=0)


def per_device(tracers, east, north, levels, partner, atm_flux, indices, weights):
    nlon, nlat = lax.axis_size("lon"), lax.axis_size("lat")
    both = ("lon", "lat")
    top = nlat - 1

    def fold_permute(rows, d):
        pairs = [(i * nlat + top, ((nlon - 1 + d - i) % nlon) * nlat + top) for i in range(nlon)]
        return lax.ppermute(rows, both, pairs)

    message = ((PLANES, H, 256), F32)
    whole_inputs = (tracers, east, north, levels, weights, indices)
    build_inputs = (*whole_inputs, atm_flux)
    first, second, fold_rows, slots = call(
        build_kernel,
        build_inputs,
        [message, message, ((10, 8, 256), F32), ((nlon * nlat, 8, 128), F32)],
        [pltpu.VMEM(a.shape, a.dtype) for a in build_inputs] + [pltpu.SemaphoreType.DMA((7,))],
        ins_any=True,
        params=pltpu.CompilerParams(vmem_limit_bytes=60 * 2**20),
    )
    def after(value, *earlier):
        return lax.optimization_barrier((value, *earlier))[0]

    swaps = [(i, i + 1) for i in range(0, nlat, 2)]
    first = lax.ppermute(first, "lat", swaps + [(j, i) for i, j in swaps])
    swaps = [(i, i + 1) for i in range(1, nlat - 1, 2)]
    swaps = [(c * nlat + i, c * nlat + j) for c in range(nlon) for i, j in swaps + [(j, i) for i, j in swaps]]
    facing = [(c * nlat + top, (nlon - 1 - c) * nlat + top) for c in range(nlon)]
    second = lax.ppermute(second, both, swaps + facing)
    fold_b = fold_permute(fold_rows, 1)

    table = lax.all_to_all(slots, both, 0, 0, tiled=True)

    partner_row = partner.reshape(1, -1)
    ghosts, to_west, to_east = call(
        pack_kernel,
        (*whole_inputs, partner_row, first, second, fold_b),
        [((80, 256), F32), ((5, 32, 128), F32), ((5, 32, 128), F32)],
    )
    from_east = lax.ppermute(to_west, "lon", [((i + 1) % nlon, i) for i in range(nlon)])
    from_west = lax.ppermute(to_east, "lon", [(i, (i + 1) % nlon) for i in range(nlon)])

    def lookups(groups, ins, splits=False, last=False, earlier=()):
        outs = [((2, 4 * len(groups), 256), F32)]
        places = ((4, 32, 256), jnp.int32)
        outs += [((512, 512), jnp.bfloat16), places, places, (places[0], F32)] if splits else []
        outs += [((2, 32, 128), F32)] if last else []
        return call(
            functools.partial(lookup_kernel, groups, splits, last), ins, outs, (), lookup_cost(len(groups)), earlier
        )

    surface_a, *places = lookups((1, 2), (table, weights, indices, first, second, ghosts), splits=True)

    wide = (2, 16, 32, 384)
    cells, fold_rows, east_ext, north_ext, depth_ext, partner_ext = call(
        first_kernel,
        (tracers, east, north, levels, partner_row, first, second, ghosts, from_east, from_west),
        [(wide, F32), ((64, 256), F32), (wide[1:], F32), (wide[1:], F32), ((32, 384), F32), ((8, 384), jnp.int32)],
        [pltpu.VMEM(wide, F32)],
        STEP_COST,
        (surface_a,),
    )
    statics = (east_ext, north_ext, depth_ext)
    received = [fold_permute(fold_rows, 0)]
    (surface_b,) = lookups((3,), places, earlier=(fold_rows,))
    received.append(fold_permute(after(fold_rows, surface_b), 1))
    (surface_c,) = lookups((4,), places, earlier=(received[0], surface_b))
    received.append(fold_permute(after(fold_rows, surface_c), -1))
    (surface_d,) = lookups((5,), places, earlier=(received[1], surface_c))
    received.append(fold_permute(after(fold_rows, surface_d), 2))
    surface_e, halo_surface = lookups((6,), (*places, from_east, from_west), last=True, earlier=(received[2], surface_d))

    ghost_rows = pltpu.VMEM((64, 384), F32)
    cells, fold_rows, surface_ext = call(
        second_kernel,
        (cells, *statics, partner_ext, *received, surface_a, surface_b, surface_c, surface_d, surface_e,
         halo_surface),
        [(wide, F32), ((64, 256), F32), ((2, 32, 384), F32)],
        [ghost_rows, pltpu.VMEM(wide, F32)],
        STEP_COST,
    )
    received = [fold_permute(fold_rows, d) for d in (0, 1, -1, 2)]
    (result,) = call(
        last_kernel,
        (cells, *statics, partner_ext, *received, surface_ext),
        [(tracers.shape, F32)],
        [ghost_rows, pltpu.VMEM(wide, F32)],
        STEP_COST,
    )
    return result


def solution(mesh):
    return jax.shard_map(
        per_device,
        mesh=mesh,
        in_specs=(
            P(None, None, "lat", "lon"),
            P(None, "lat", "lon"),
            P(None, "lat", "lon"),
            P("lat", "lon"),
            P("lon"),
            P(None, ("lon", "lat")),
            P(None, "lat", "lon"),
            P(None, "lat", "lon"),
        ),
        out_specs=P(None, None, "lat", "lon"),
        check_vma=False,
    )
```
